512 devices in a mesh: resp: 16 (over y_hi, z), heads: 8 (over x, core), prompt: 4 (over y_lo).
Axes of the slice: x: 4, y: 8 (y_hi: 2, y_lo: 4; y = y_hi * 4 + y_lo), z: 8, core: 2. Of those that a mesh axis runs over, the one named last changes fastest.
Arguments:
- queries: bfloat16 [64, 512, 8192], P(('resp', 'prompt'), 'heads'), may hold values from -8 to 8
- outputs: bfloat16 [64, 512, 8192], P(('resp', 'prompt'), 'heads'), may hold values from -6 to 6
- out_grads: bfloat16 [64, 512, 8192], P(('resp', 'prompt'), 'heads'), may hold values from -24 to 24
- resp_keys: bfloat16 [64, 512, 1024], P(('resp', 'prompt'), 'heads'), may hold values from -6 to 6
- resp_values: bfloat16 [64, 512, 1024], P(('resp', 'prompt'), 'heads'), may hold values from -6 to 6
- prompt_keys: bfloat16 [512, 4, 1024], P(('resp', 'prompt'), None, 'heads'), may hold values from -8 to 8
- prompt_values: bfloat16 [512, 4, 1024], P(('resp', 'prompt'), None, 'heads'), may hold values from -6 to 6
- prompt_of: int32 [64], P(('resp', 'prompt')), may hold values from 0 to 3
- lengths: int32 [64], P(('resp', 'prompt')), may hold values from 64 to 512, as said below
Outputs:
- query_grads: bfloat16 [64, 512, 8192], P(('resp', 'prompt'), 'heads')
- resp_key_grads: bfloat16 [64, 512, 1024], P(('resp', 'prompt'), 'heads')
- resp_value_grads: bfloat16 [64, 512, 1024], P(('resp', 'prompt'), 'heads')
- prompt_key_grads: bfloat16 [512, 4, 1024], P(('resp', 'prompt'), None, 'heads')
- prompt_value_grads: bfloat16 [512, 4, 1024], P(('resp', 'prompt'), None, 'heads')
The draws below stay inside these ranges and needn't reach their ends.
Inputs may be any that keep to these rules, and one draw needn't show every extreme that they name: `lengths`: some response has exactly 512 live tokens.
All inputs are finite; a program needn't handle non-finite values.
Results may differ from the reference program's by a relative error of at most 0.0055.
Values may be sent and summed in bfloat16 or wider, within the bound.
A program may use at most 64 MiB of HBM per device.

```python
import jax
import jax.numpy as jnp
from jax import lax

HD = 128
NQH = 64
NKVH = 8
NPROMPT = 4
RLEN = 512
PLEN = 512
RESPONSES = 64


def draw_queries(key, part):
    key = jax.random.fold_in(key, 1)
    values = jax.random.normal(jax.random.fold_in(key, 11), (RESPONSES, RLEN, NQH * HD), jnp.float32)
    values = jnp.clip(values, -8.0, 8.0)
    return values.astype(jnp.bfloat16)


def draw_prompt_keys(key, part):
    key = jax.random.fold_in(key, 2)
    values = jax.random.normal(jax.random.fold_in(key, 21), (PLEN, NPROMPT, NKVH * HD), jnp.float32)
    values = jnp.clip(values, -8.0, 8.0)
    return values.astype(jnp.bfloat16)


def draw_lengths(key, part):
    key = jax.random.fold_in(key, 4)
    lens = jax.random.randint(jax.random.fold_in(key, 41), (RESPONSES,), RLEN // 8, RLEN + 1)
    spot = jax.random.randint(jax.random.fold_in(key, 42), (), 0, RESPONSES)
    return lens.at[spot].set(RLEN).astype(jnp.int32)


def touch_ends(values, own_key, smallest, largest):
    longest = values.shape.index(max(values.shape))
    spots = []
    for shift in (0, 1):
        where = [jax.random.randint(jax.random.fold_in(own_key, axis), (), 0, length) for axis, length in enumerate(values.shape)]
        where[longest] = (where[longest] + shift) % values.shape[longest]
        spots.append(tuple(where))
    return values.at[spots[0]].set(smallest).at[spots[1]].set(largest)


def shard_levels(stream_key, dims, shards, smallest, top_value):
    def one(dim, shards_of):
        heights = jax.random.uniform(jax.random.fold_in(jax.random.fold_in(stream_key, 6), dim), (shards_of,), jnp.float32, smallest / len(shards), top_value / len(shards))
        return jnp.repeat(jnp.exp(heights), dims[dim] // shards_of).reshape((-1,) + (1,) * (len(dims) - dim - 1))

    gain = one(*shards[0])
    for cut in shards[1:]:
        gain = gain * one(*cut)
    return gain


def normal_values(stream_key, dims, scale, most, split=(), held_as=jnp.bfloat16):
    array = jax.random.normal(stream_key, dims, jnp.float32) * scale
    if len(split) > 0:
        array = shard_levels(stream_key, dims, split, -0.22, 0.18) * array
    return jnp.clip(array, min=-most, max=most).astype(held_as)


def setup_inputs(seed: int = 0) -> dict:
    arg_keys = jax.random.split(jax.random.key(seed), 10)
    queries = draw_queries(jax.random.fold_in(arg_keys[9], 71), 0)
    outputs = normal_values(arg_keys[1], (RESPONSES, RLEN, NQH * HD), 1.0, 6.0, ((0, 64), (1, 8)))
    out_grads = normal_values(arg_keys[2], (RESPONSES, RLEN, NQH * HD), 4.0, 24.0, ((0, 64), (1, 8)))
    resp_keys = normal_values(arg_keys[3], (RESPONSES, RLEN, NKVH * HD), 1.0, 6.0, ((0, 64), (1, 8)))
    resp_values = normal_values(arg_keys[4], (RESPONSES, RLEN, NKVH * HD), 1.0, 6.0, ((0, 64), (1, 8)))
    prompt_keys = draw_prompt_keys(jax.random.fold_in(arg_keys[9], 71), 0)
    prompt_values = normal_values(arg_keys[6], (PLEN, NPROMPT, NKVH * HD), 1.0, 6.0, ((0, 64), (2, 8)))
    prompt_of = touch_ends(jax.random.randint(arg_keys[7], (RESPONSES,), 0, NPROMPT), jax.random.fold_in(arg_keys[7], 1), 0, NPROMPT - 1).astype(jnp.int32)
    lengths = draw_lengths(jax.random.fold_in(arg_keys[9], 71), 0)
    return {"queries": queries, "outputs": outputs, "out_grads": out_grads, "resp_keys": resp_keys, "resp_values": resp_values, "prompt_keys": prompt_keys, "prompt_values": prompt_values, "prompt_of": prompt_of, "lengths": lengths}


def response_grads(queries_r, outputs_r, grads_r, live_rows, key_prompt, value_prompt, key_own, value_own):
    wide = jnp.float32
    scale = HD ** -0.5
    query_f = queries_r.astype(wide)
    grad_live = jnp.where(live_rows[:, None, None, None], grads_r, jnp.zeros_like(grads_r)).astype(wide)
    score_p = scale * jnp.einsum('rkgd,pkd->kgrp', query_f, key_prompt.astype(wide))
    score_r = scale * jnp.einsum('rkgd,jkd->kgrj', query_f, key_own.astype(wide))
    causal = jnp.arange(RLEN)[:, None] >= jnp.arange(RLEN)[None, :]
    score_r = jnp.where(causal, score_r, -jnp.inf)
    peak = jnp.maximum(jnp.max(score_p, -1), jnp.max(score_r, -1))
    total = jnp.sum(jnp.exp(score_p - peak[..., None]), -1) + jnp.sum(jnp.exp(score_r - peak[..., None]), -1)
    log_total = peak + jnp.log(total)
    prob_p = jnp.exp(score_p - log_total[..., None])
    prob_r = jnp.exp(score_r - log_total[..., None])
    delta = jnp.einsum('rkgd,rkgd->kgr', grad_live, outputs_r.astype(wide))
    dprob_p = jnp.einsum('rkgd,pkd->kgrp', grad_live, value_prompt.astype(wide))
    dprob_r = jnp.einsum('rkgd,jkd->kgrj', grad_live, value_own.astype(wide))
    dscore_p = lax.optimization_barrier((prob_p * (dprob_p - delta[..., None])).astype(jnp.bfloat16)).astype(wide)
    dscore_r = lax.optimization_barrier((prob_r * (dprob_r - delta[..., None])).astype(jnp.bfloat16)).astype(wide)
    prob_pb = lax.optimization_barrier(prob_p.astype(jnp.bfloat16)).astype(wide)
    prob_rb = lax.optimization_barrier(prob_r.astype(jnp.bfloat16)).astype(wide)
    dquery = scale * (jnp.einsum('kgrp,pkd->rkgd', dscore_p, key_prompt.astype(wide)) + jnp.einsum('kgrj,jkd->rkgd', dscore_r, key_own.astype(wide)))
    dkey_p = scale * jnp.einsum('kgrp,rkgd->pkd', dscore_p, query_f)
    dval_p = jnp.einsum('kgrp,rkgd->pkd', prob_pb, grad_live)
    dkey_r = scale * jnp.einsum('kgrj,rkgd->jkd', dscore_r, query_f)
    dval_r = jnp.einsum('kgrj,rkgd->jkd', prob_rb, grad_live)
    return dquery, dkey_p, dval_p, dkey_r, dval_r


def reference(queries, outputs, out_grads, resp_keys, resp_values, prompt_keys, prompt_values, prompt_of, lengths):
    group = NQH // NKVH
    key_all = prompt_keys.reshape(PLEN, NPROMPT, NKVH, HD)
    value_all = prompt_values.reshape(PLEN, NPROMPT, NKVH, HD)

    def visit(terms, index):
        term_k, term_v = terms
        prompt_id = prompt_of[index]
        queries_r = queries[index].reshape(RLEN, NKVH, group, HD)
        outputs_r = outputs[index].reshape(RLEN, NKVH, group, HD)
        grads_r = out_grads[index].reshape(RLEN, NKVH, group, HD)
        key_own = resp_keys[index].reshape(RLEN, NKVH, HD)
        value_own = resp_values[index].reshape(RLEN, NKVH, HD)
        key_prompt = lax.dynamic_index_in_dim(key_all, prompt_id, 1, keepdims=False)
        value_prompt = lax.dynamic_index_in_dim(value_all, prompt_id, 1, keepdims=False)
        live_rows = jnp.arange(RLEN, dtype=jnp.int32) < lengths[index]
        dquery, dkey_p, dval_p, dkey_r, dval_r = response_grads(queries_r, outputs_r, grads_r, live_rows, key_prompt, value_prompt, key_own, value_own)
        onehot = (jnp.arange(NPROMPT, dtype=jnp.int32) == prompt_id).astype(jnp.float32)
        term_k = term_k + onehot[None, :, None, None] * dkey_p[:, None]
        term_v = term_v + onehot[None, :, None, None] * dval_p[:, None]
        shaped = (dquery.astype(jnp.bfloat16).reshape(RLEN, NQH * HD), dkey_r.astype(jnp.bfloat16).reshape(RLEN, NKVH * HD), dval_r.astype(jnp.bfloat16).reshape(RLEN, NKVH * HD))
        return (term_k, term_v), shaped

    empty = jnp.zeros((PLEN, NPROMPT, NKVH, HD), jnp.float32)
    terms, shaped = lax.scan(visit, (empty, empty), jnp.arange(RESPONSES, dtype=jnp.int32))
    prompt_dk = terms[0].reshape(PLEN, NPROMPT, NKVH * HD).astype(jnp.bfloat16)
    prompt_dv = terms[1].reshape(PLEN, NPROMPT, NKVH * HD).astype(jnp.bfloat16)
    return (shaped[0], shaped[1], shaped[2], prompt_dk, prompt_dv)
```

```python
import functools

import jax
import jax.numpy as jnp
from jax import lax
from jax.experimental import pallas as pl
from jax.experimental.pallas import tpu as pltpu
from jax.sharding import PartitionSpec as P

HD = 128
LOG2E = 1.4426950408889634
WIDE = jnp.float32
HALF = jnp.bfloat16
NT = (((1,), (1,)), ((), ()))
NN = (((1,), (0,)), ((), ()))


def dot(a, b, dims):
    return lax.dot_general(a, b, dims, preferred_element_type=WIDE)


def kernel(
    sizes,
    prompt_id,
    length,
    q_in,
    o_in,
    g_in,
    k_in,
    v_in,
    pkv_in,
    dq_out,
    dk_out,
    dv_out,
    dpkv_out,
    q_all,
    g_all,
    k_all,
    v_all,
    o_mine,
    g_mine,
    delta_send,
    delta_all,
    id_send,
    id_all,
    quarter,
    chosen,
    pkv_all,
    kt,
    pkt,
    dq_all,
    dk_acc,
    dv_acc,
    dpk_acc,
    dpv_acc,
    dk_half,
    dv_half,
    term_send,
    term_all,
    dense,
    dense_all,
    send,
    recv_id,
    recv_quarter,
    recv_pkv,
    recv_kv,
    recv_delta,
    recv_q,
    recv_g,
    recv_dq,
    recv_dkv,
    recv_term,
    recv_dense,
    local,
):
    heads, resps, prompts, group, rows, stages, row_block, own_tokens, prompt_count = sizes
    me = lax.axis_index("heads")
    mine_r = lax.axis_index("resp")
    mine_p = lax.axis_index("prompt")
    total_rows = heads * rows
    width = group * HD
    per_stage = group // stages
    stage_width = per_stage * HD
    span = own_tokens * prompts
    scale = HD**-0.5

    def start(src, dst, send_sem, recv_sem, axis, index):
        pltpu.make_async_remote_copy(
            src_ref=src,
            dst_ref=dst,
            send_sem=send_sem,
            recv_sem=recv_sem,
            device_id={axis: index},
            device_id_type=pl.DeviceIdType.MESH,
        ).start()

    def landed(ref, sem):
        pltpu.make_async_copy(ref, ref, sem).wait()

    def others(count, own, body):
        def step(i, carry):
            body(lax.rem(own + i, count))
            return carry

        lax.fori_loop(1, count, step, 0)

    load_o = pltpu.make_async_copy(o_in, o_mine, local.at[0])
    load_g = pltpu.make_async_copy(g_in, g_mine, local.at[1])
    load_o.start()
    load_g.start()
    own_cols = pl.ds(pl.multiple_of(me * width, width), width)
    own_rows = pl.ds(pl.multiple_of(me * rows, rows), rows)
    own_head = pl.ds(pl.multiple_of(me * HD, HD), HD)
    keep = [
        pltpu.make_async_copy(q_in.at[:, own_cols], q_all.at[own_rows, :], local.at[2]),
        pltpu.make_async_copy(g_in.at[:, own_cols], g_all.at[own_rows, :], local.at[3]),
        pltpu.make_async_copy(k_in.at[:, own_head], k_all.at[own_rows, :], local.at[4]),
        pltpu.make_async_copy(v_in.at[:, own_head], v_all.at[own_rows, :], local.at[5]),
    ]
    for copy in keep:
        copy.start()

    barrier = pltpu.get_barrier_semaphore()
    for axis, count, own in (("heads", heads, me), ("resp", resps, mine_r), ("prompt", prompts, mine_p)):

        def greet(peer, axis=axis):
            pl.semaphore_signal(
                barrier, inc=1, device_id={axis: peer}, device_id_type=pl.DeviceIdType.MESH
            )

        others(count, own, greet)
    id_tile = jnp.full((8, HD), prompt_id[0], jnp.int32).astype(WIDE)
    id_send[...] = id_tile
    id_all[mine_r] = id_tile
    quarter[mine_p] = pkv_in[...]
    pl.semaphore_wait(barrier, heads + resps + prompts - 3)

    others(resps, mine_r, lambda p: start(id_send, id_all.at[mine_r], send.at[0], recv_id, "resp", p))
    others(
        prompts,
        mine_p,
        lambda p: start(pkv_in, quarter.at[mine_p], send.at[1], recv_quarter, "prompt", p),
    )

    def send_kv(p):
        cols = pl.ds(pl.multiple_of(p * HD, HD), HD)
        start(k_in.at[:, cols], k_all.at[own_rows, :], send.at[2], recv_kv.at[0], "heads", p)
        start(v_in.at[:, cols], v_all.at[own_rows, :], send.at[3], recv_kv.at[1], "heads", p)

    others(heads, me, send_kv)

    def send_stage(stage):
        to = pl.ds(pl.multiple_of(stage * stage_width, stage_width), stage_width)

        def body(p):
            cols = pl.ds(pl.multiple_of(p * width + stage * stage_width, stage_width), stage_width)
            start(q_in.at[:, cols], q_all.at[own_rows, to], send.at[4], recv_q.at[stage], "heads", p)
            start(g_in.at[:, cols], g_all.at[own_rows, to], send.at[5], recv_g.at[stage], "heads", p)

        others(heads, me, body)

    send_stage(0)

    landed(quarter.at[pl.ds(0, prompts - 1)], recv_quarter)
    landed(id_all.at[pl.ds(0, resps - 1)], recv_id)
    held = [quarter[b].astype(WIDE) for b in range(prompts)]
    part = prompt_count * own_tokens

    def pick(kv, c):
        lo = kv * part + c * own_tokens
        return jnp.concatenate([h[lo : lo + own_tokens] for h in held], axis=0)

    by_prompt = [jnp.concatenate([pick(0, c), pick(1, c)], axis=0) for c in range(prompt_count)]

    def weights(index):
        return [(id_all[index] == float(c)).astype(WIDE)[0:1] for c in range(prompt_count)]

    def choose(p):
        w = weights(p)
        out = w[0] * by_prompt[0]
        for c in range(1, prompt_count):
            out = out + w[c] * by_prompt[c]
        return out.astype(HALF)

    def send_prompt(p):
        chosen[p] = choose(p)
        start(chosen.at[p], pkv_all.at[mine_r], send.at[6], recv_pkv, "resp", p)

    others(resps, mine_r, send_prompt)
    pkv_all[mine_r] = choose(mine_r)

    load_o.wait()
    load_g.wait()
    head_of = lax.broadcasted_iota(jnp.int32, (group, width), 1) // HD
    ones = (head_of == lax.broadcasted_iota(jnp.int32, (group, width), 0)).astype(HALF)
    side = lax.rem(me, 2)
    first = (lax.broadcasted_iota(jnp.int32, (group, 2 * rows), 1) // rows) == side

    def delta_for(p):
        cols = pl.ds(pl.multiple_of(p * width, width), width)
        prod = o_mine[:, cols].astype(WIDE) * g_mine[:, cols].astype(WIDE)
        high = prod.astype(HALF)
        low = (prod - high.astype(WIDE)).astype(HALF)
        d = dot(ones, high, NT) + dot(ones, low, NT)
        return jnp.where(first, jnp.concatenate([d, d], axis=1), 0.0)

    def send_delta(p):
        delta_send[p] = delta_for(p)
        start(delta_send.at[p], delta_all.at[me], send.at[7], recv_delta, "heads", p)

    others(heads, me, send_delta)
    delta_all[me] = delta_for(me)

    def rest(stage, carry):
        send_stage(stage)
        return carry

    lax.fori_loop(1, stages, rest, 0)

    dk_acc[...] = jnp.zeros_like(dk_acc)
    dv_acc[...] = jnp.zeros_like(dv_acc)
    dpk_acc[...] = jnp.zeros_like(dpk_acc)
    dpv_acc[...] = jnp.zeros_like(dpv_acc)
    for copy in keep:
        copy.wait()
    landed(k_all.at[pl.ds(0, total_rows - rows)], recv_kv.at[0])
    landed(v_all.at[pl.ds(0, total_rows - rows)], recv_kv.at[1])
    landed(delta_all.at[pl.ds(0, heads - 1)], recv_delta)
    landed(pkv_all.at[pl.ds(0, resps - 1)], recv_pkv)
    prompt_len = resps * span
    kt[...] = k_all[...].T
    pkt[...] = pkv_all[:, 0:span, :].reshape(prompt_len, HD).T
    delta_rows = jnp.concatenate(
        [delta_all[2 * i] + delta_all[2 * i + 1] for i in range(heads // 2)], axis=1
    )
    live = (lax.broadcasted_iota(jnp.int32, (1, total_rows), 1) < length[0]).astype(WIDE)
    causal = lax.broadcasted_iota(jnp.int32, (row_block, row_block), 0) <= lax.broadcasted_iota(
        jnp.int32, (row_block, row_block), 1
    )

    def one_block(head_in_group, delta_head, block):
        cols = pl.ds(pl.multiple_of(head_in_group * HD, HD), HD)
        lo = block * row_block
        at = slice(lo, lo + row_block)
        keys = lo + row_block
        q = q_all[lo : lo + row_block, cols]
        g = g_all[lo : lo + row_block, cols]
        pk = pkv_all[:, 0:span, :].reshape(prompt_len, HD)
        pv = pkv_all[:, span : 2 * span, :].reshape(prompt_len, HD)
        score_p = dot(pk, q, NT)
        score_r = dot(k_all[0:keys, :], q, NT)
        diag = jnp.where(causal, score_r[lo:keys], -jnp.inf)
        score_r = diag if lo == 0 else jnp.concatenate([score_r[0:lo], diag], axis=0)
        peak = jnp.maximum(
            jnp.max(score_p, axis=0, keepdims=True), jnp.max(score_r, axis=0, keepdims=True)
        )
        e_p = jnp.exp2((score_p - peak) * (scale * LOG2E))
        e_r = jnp.exp2((score_r - peak) * (scale * LOG2E))
        total = jnp.sum(e_p, axis=0, keepdims=True) + jnp.sum(e_r, axis=0, keepdims=True)
        norm = live[:, at] / total
        prob_p = e_p * norm
        prob_r = e_r * norm
        d = delta_head[:, at]
        ds_p = (prob_p * (dot(pv, g, NT) - d)).astype(HALF)
        ds_r = (prob_r * (dot(v_all[0:keys, :], g, NT) - d)).astype(HALF)
        prob_p = prob_p.astype(HALF)
        prob_r = prob_r.astype(HALF)
        dpv_acc[...] += dot(prob_p, g, NN)
        dv_acc[0:keys, :] += dot(prob_r, g, NN)
        dpk_acc[...] += dot(ds_p, q, NN)
        dk_acc[0:keys, :] += dot(ds_r, q, NN)
        dq_t = dot(pkt[...], ds_p, NN) + dot(kt[:, 0:keys], ds_r, NN)
        dq_all[lo : lo + row_block, cols] = (dq_t * scale).T.astype(HALF)

    def visit(stage, carry):
        landed(q_all.at[pl.ds(0, total_rows - rows), pl.ds(0, stage_width)], recv_q.at[stage])
        landed(g_all.at[pl.ds(0, total_rows - rows), pl.ds(0, stage_width)], recv_g.at[stage])
        for sub in range(per_stage):
            head_in_group = stage * per_stage + sub
            pick_head = (
                lax.broadcasted_iota(jnp.int32, (group, total_rows), 0) == head_in_group
            ).astype(WIDE)
            delta_head = jnp.sum(delta_rows * pick_head, axis=0, keepdims=True)
            for block in range(total_rows // row_block):
                one_block(head_in_group, delta_head, block)
        src_cols = pl.ds(pl.multiple_of(stage * stage_width, stage_width), stage_width)
        dst_cols = pl.ds(pl.multiple_of(me * width + stage * stage_width, stage_width), stage_width)

        def give(p):
            part_rows = pl.ds(pl.multiple_of(p * rows, rows), rows)
            start(
                dq_all.at[part_rows, src_cols],
                dq_out.at[:, dst_cols],
                send.at[8],
                recv_dq,
                "heads",
                p,
            )

        others(heads, me, give)
        return carry

    lax.fori_loop(0, stages, visit, 0)

    for a in range(resps):
        lo = a * span
        term_send[a] = jnp.concatenate(
            [dpk_acc[lo : lo + span, :] * scale, dpv_acc[lo : lo + span, :]], axis=0
        ).astype(HALF)
    others(
        resps,
        mine_r,
        lambda p: start(term_send.at[p], term_all.at[mine_r], send.at[9], recv_term, "resp", p),
    )
    dk_half[...] = (dk_acc[...] * scale).astype(HALF)
    dv_half[...] = dv_acc[...].astype(HALF)

    def give_own(p):
        part_rows = pl.ds(pl.multiple_of(p * rows, rows), rows)
        start(dk_half.at[part_rows, :], dk_out.at[:, own_head], send.at[10], recv_dkv.at[0], "heads", p)
        start(dv_half.at[part_rows, :], dv_out.at[:, own_head], send.at[11], recv_dkv.at[1], "heads", p)

    others(heads, me, give_own)
    put = [
        pltpu.make_async_copy(dq_all.at[own_rows, :], dq_out.at[:, own_cols], local.at[0]),
        pltpu.make_async_copy(dk_half.at[own_rows, :], dk_out.at[:, own_head], local.at[1]),
        pltpu.make_async_copy(dv_half.at[own_rows, :], dv_out.at[:, own_head], local.at[2]),
    ]
    for copy in put:
        copy.start()
    term_all[mine_r] = term_send[mine_r]
    landed(term_all.at[pl.ds(0, resps - 1)], recv_term)
    sums = [jnp.zeros((2 * span, HD), WIDE) for c in range(prompt_count)]
    for a in range(resps):
        w = weights(a)
        term = term_all[a].astype(WIDE)
        sums = [s + w[c] * term for c, s in enumerate(sums)]
    for b in range(prompts):
        pieces = []
        for kv in range(2):
            for c in range(prompt_count):
                lo = kv * span + b * own_tokens
                pieces.append(sums[c][lo : lo + own_tokens])
        dense[b] = jnp.concatenate(pieces, axis=0)
    dense_all[mine_p] = dense[mine_p]
    others(
        prompts,
        mine_p,
        lambda p: start(dense.at[p], dense_all.at[mine_p], send.at[12], recv_dense, "prompt", p),
    )
    landed(dense_all.at[pl.ds(0, prompts - 1)], recv_dense)
    result = dense_all[0]
    for b in range(1, prompts):
        result = result + dense_all[b]
    dpkv_out[...] = result

    for copy in put:
        copy.wait()
    far = pl.ds(0, (heads - 1) * width)
    far_kv = pl.ds(0, (heads - 1) * HD)
    landed(dq_out.at[:, far], recv_dq)
    landed(dk_out.at[:, far_kv], recv_dkv.at[0])
    landed(dv_out.at[:, far_kv], recv_dkv.at[1])
    landed(id_all.at[pl.ds(0, resps - 1)], send.at[0])
    landed(quarter.at[pl.ds(0, prompts - 1)], send.at[1])
    landed(k_all.at[pl.ds(0, total_rows - rows)], send.at[2])
    landed(v_all.at[pl.ds(0, total_rows - rows)], send.at[3])
    landed(q_all.at[pl.ds(0, total_rows - rows)], send.at[4])
    landed(g_all.at[pl.ds(0, total_rows - rows)], send.at[5])
    landed(chosen.at[pl.ds(0, resps - 1)], send.at[6])
    landed(delta_all.at[pl.ds(0, heads - 1)], send.at[7])
    landed(dq_all.at[pl.ds(0, total_rows - rows)], send.at[8])
    landed(term_all.at[pl.ds(0, resps - 1)], send.at[9])
    landed(dk_half.at[pl.ds(0, total_rows - rows)], send.at[10])
    landed(dv_half.at[pl.ds(0, total_rows - rows)], send.at[11])
    landed(dense_all.at[pl.ds(0, prompts - 1)], send.at[12])


def on_device(
    mesh_sizes,
    queries,
    outputs,
    out_grads,
    resp_keys,
    resp_values,
    prompt_keys,
    prompt_values,
    prompt_of,
    lengths,
):
    heads, resps, prompts = mesh_sizes
    rows = queries.shape[1]
    kv_heads = resp_keys.shape[2] // HD
    group = queries.shape[2] // HD // kv_heads
    own_tokens, prompt_count = prompt_keys.shape[:2]
    total_rows = heads * rows
    stages = 4
    row_block = total_rows // 2
    span = own_tokens * prompts
    prompt_len = span * resps
    width = group * HD
    sizes = (heads, resps, prompts, group, rows, stages, row_block, own_tokens, prompt_count)

    pkv = jnp.concatenate(
        [
            prompt_keys.transpose(1, 0, 2).reshape(own_tokens * prompt_count, HD),
            prompt_values.transpose(1, 0, 2).reshape(own_tokens * prompt_count, HD),
        ],
        axis=0,
    )
    both = 2 * own_tokens * prompt_count
    vmem = pltpu.VMEM
    dma = pltpu.SemaphoreType.DMA
    hbm = pl.BlockSpec(memory_space=pl.ANY)
    smem = pl.BlockSpec(memory_space=pltpu.SMEM)
    in_vmem = pl.BlockSpec(memory_space=pltpu.VMEM)
    dq, dk, dv, dpkv = pl.pallas_call(
        functools.partial(kernel, sizes),
        out_shape=(
            jax.ShapeDtypeStruct((rows, queries.shape[2]), HALF),
            jax.ShapeDtypeStruct((rows, resp_keys.shape[2]), HALF),
            jax.ShapeDtypeStruct((rows, resp_keys.shape[2]), HALF),
            jax.ShapeDtypeStruct((both, HD), WIDE),
        ),
        in_specs=[smem, smem, hbm, hbm, hbm, hbm, hbm, in_vmem],
        out_specs=(hbm, hbm, hbm, in_vmem),
        scratch_shapes=[
            vmem((total_rows, width), HALF),
            vmem((total_rows, width), HALF),
            vmem((total_rows, HD), HALF),
            vmem((total_rows, HD), HALF),
            vmem((rows, queries.shape[2]), HALF),
            vmem((rows, queries.shape[2]), HALF),
            vmem((heads, group, 2 * rows), WIDE),
            vmem((heads, group, 2 * rows), WIDE),
            vmem((8, HD), WIDE),
            vmem((resps, 8, HD), WIDE),
            vmem((prompts, both, HD), HALF),
            vmem((resps, 2 * span, HD), HALF),
            vmem((resps, 2 * span, HD), HALF),
            vmem((HD, total_rows), HALF),
            vmem((HD, prompt_len), HALF),
            vmem((total_rows, width), HALF),
            vmem((total_rows, HD), WIDE),
            vmem((total_rows, HD), WIDE),
            vmem((prompt_len, HD), WIDE),
            vmem((prompt_len, HD), WIDE),
            vmem((total_rows, HD), HALF),
            vmem((total_rows, HD), HALF),
            vmem((resps, 2 * span, HD), HALF),
            vmem((resps, 2 * span, HD), HALF),
            vmem((prompts, both, HD), WIDE),
            vmem((prompts, both, HD), WIDE),
            dma((13,)),
            dma,
            dma,
            dma,
            dma((2,)),
            dma,
            dma((stages,)),
            dma((stages,)),
            dma,
            dma((2,)),
            dma,
            dma,
            dma((6,)),
        ],
        compiler_params=pltpu.CompilerParams(
            collective_id=0, has_side_effects=True, vmem_limit_bytes=48 * 1024 * 1024
        ),
    )(
        prompt_of,
        lengths,
        queries[0],
        outputs[0],
        out_grads[0],
        resp_keys[0],
        resp_values[0],
        pkv,
    )
    dp = dpkv.reshape(2, prompt_count, own_tokens, HD).transpose(0, 2, 1, 3).astype(HALF)
    return dq[None], dk[None], dv[None], dp[0], dp[1]


def solution(mesh):
    sizes = (mesh.shape["heads"], mesh.shape["resp"], mesh.shape["prompt"])
    return jax.shard_map(
        functools.partial(on_device, sizes),
        mesh=mesh,
        in_specs=(
            P(("resp", "prompt"), "heads", None),
            P(("resp", "prompt"), "heads", None),
            P(("resp", "prompt"), "heads", None),
            P(("resp", "prompt"), "heads", None),
            P(("resp", "prompt"), "heads", None),
            P(("resp", "prompt"), None, "heads"),
            P(("resp", "prompt"), None, "heads"),
            P(("resp", "prompt")),
            P(("resp", "prompt")),
        ),
        out_specs=(
            P(("resp", "prompt"), "heads", None),
            P(("resp", "prompt"), "heads", None),
            P(("resp", "prompt"), "heads", None),
            P(("resp", "prompt"), None, "heads"),
            P(("resp", "prompt"), None, "heads"),
        ),
        check_vma=False,
    )
```

```python
import functools

import jax
import jax.numpy as jnp
from jax import lax
from jax.experimental import pallas as pl
from jax.experimental.pallas import tpu as pltpu
from jax.sharding import PartitionSpec as P

HD = 128
LOG2E = 1.4426950408889634
WIDE = jnp.float32
HALF = jnp.bfloat16
NT = (((1,), (1,)), ((), ()))
NN = (((1,), (0,)), ((), ()))


def dot(a, b, dims):
    return lax.dot_general(a, b, dims, preferred_element_type=WIDE)


def kernel(
    sizes,
    prompt_id,
    length,
    q_in,
    o_in,
    g_in,
    k_in,
    v_in,
    pk_in,
    pv_in,
    dq_out,
    dkv_out,
    dpkv_out,
    q_all,
    g_all,
    k_all,
    v_all,
    q_mine,
    o_mine,
    g_mine,
    k_mine,
    v_mine,
    pk_mine,
    pv_mine,
    delta_send,
    delta_all,
    id_send,
    id_all,
    pkv_send,
    quarter,
    chosen,
    pkv_all,
    kt,
    pkt,
    dq_all,
    dk_acc,
    dv_acc,
    dpk_acc,
    dpv_acc,
    dk_half,
    dv_half,
    term_send,
    term_all,
    dense,
    dense_all,
    send,
    recv_id,
    recv_quarter,
    recv_pkv,
    recv_kv,
    recv_delta,
    recv_q,
    recv_g,
    recv_dq,
    recv_dkv,
    recv_term,
    recv_dense,
    local,
):
    heads, resps, prompts, group, rows, stages, row_block, own_tokens, prompt_count = sizes
    me = lax.axis_index("heads")
    mine_r = lax.axis_index("resp")
    mine_p = lax.axis_index("prompt")
    total_rows = heads * rows
    width = group * HD
    per_stage = group // stages
    stage_width = per_stage * HD
    span = own_tokens * prompts
    scale = HD**-0.5

    def start(src, dst, send_sem, recv_sem, axis, index):
        pltpu.make_async_remote_copy(
            src_ref=src,
            dst_ref=dst,
            send_sem=send_sem,
            recv_sem=recv_sem,
            device_id={axis: index},
            device_id_type=pl.DeviceIdType.MESH,
        ).start()

    def landed(ref, sem):
        pltpu.make_async_copy(ref, ref, sem).wait()

    def others(count, own, body):
        def step(i, carry):
            body(lax.rem(own + i, count))
            return carry

        lax.fori_loop(1, count, step, 0)

    loads = [
        pltpu.make_async_copy(src, dst, local.at[n])
        for n, (src, dst) in enumerate(
            (
                (pk_in, pk_mine),
                (pv_in, pv_mine),
                (k_in, k_mine),
                (v_in, v_mine),
                (q_in, q_mine),
                (g_in, g_mine),
                (o_in, o_mine),
            )
        )
    ]
    for copy in loads:
        copy.start()
    own_cols = pl.ds(pl.multiple_of(me * width, width), width)
    own_rows = pl.ds(pl.multiple_of(me * rows, rows), rows)
    own_head = pl.ds(pl.multiple_of(me * HD, HD), HD)

    barrier = pltpu.get_barrier_semaphore()
    for axis, count, own in (("heads", heads, me), ("resp", resps, mine_r), ("prompt", prompts, mine_p)):

        def greet(peer, axis=axis):
            pl.semaphore_signal(
                barrier, inc=1, device_id={axis: peer}, device_id_type=pl.DeviceIdType.MESH
            )

        others(count, own, greet)
    for copy in loads[:2]:
        copy.wait()
    id_tile = jnp.full((8, HD), prompt_id[0], jnp.int32).astype(WIDE)
    id_send[...] = id_tile
    id_all[mine_r] = id_tile
    mine_k = pk_mine[...].astype(WIDE)
    mine_v = pv_mine[...].astype(WIDE)
    pkv_send[...] = jnp.concatenate(
        [mine_k[:, c, :] for c in range(prompt_count)]
        + [mine_v[:, c, :] for c in range(prompt_count)],
        axis=0,
    ).astype(HALF)
    quarter[mine_p] = pkv_send[...]
    for copy in loads[2:]:
        copy.wait()
    pl.semaphore_wait(barrier, heads + resps + prompts - 3)

    others(resps, mine_r, lambda p: start(id_send, id_all.at[mine_r], send.at[0], recv_id, "resp", p))
    others(
        prompts,
        mine_p,
        lambda p: start(pkv_send, quarter.at[mine_p], send.at[1], recv_quarter, "prompt", p),
    )

    def send_kv(p):
        cols = pl.ds(pl.multiple_of(p * HD, HD), HD)
        start(k_mine.at[:, cols], k_all.at[own_rows, :], send.at[2], recv_kv.at[0], "heads", p)
        start(v_mine.at[:, cols], v_all.at[own_rows, :], send.at[3], recv_kv.at[1], "heads", p)

    others(heads, me, send_kv)
    k_all[own_rows, :] = k_mine[:, own_head]
    v_all[own_rows, :] = v_mine[:, own_head]

    def send_stage(stage):
        to = pl.ds(pl.multiple_of(stage * stage_width, stage_width), stage_width)

        def body(p):
            cols = pl.ds(pl.multiple_of(p * width + stage * stage_width, stage_width), stage_width)
            start(q_mine.at[:, cols], q_all.at[own_rows, to], send.at[4], recv_q.at[stage], "heads", p)
            start(g_mine.at[:, cols], g_all.at[own_rows, to], send.at[5], recv_g.at[stage], "heads", p)

        others(heads, me, body)

    send_stage(0)

    landed(quarter.at[pl.ds(0, prompts - 1)], recv_quarter)
    landed(id_all.at[pl.ds(0, resps - 1)], recv_id)
    held = [quarter[b].astype(WIDE) for b in range(prompts)]
    part = prompt_count * own_tokens

    def pick(kv, c):
        lo = kv * part + c * own_tokens
        return jnp.concatenate([h[lo : lo + own_tokens] for h in held], axis=0)

    by_prompt = [jnp.concatenate([pick(0, c), pick(1, c)], axis=0) for c in range(prompt_count)]

    def weights(index):
        return [(id_all[index] == float(c)).astype(WIDE)[0:1] for c in range(prompt_count)]

    def choose(p):
        w = weights(p)
        out = w[0] * by_prompt[0]
        for c in range(1, prompt_count):
            out = out + w[c] * by_prompt[c]
        return out.astype(HALF)

    def send_prompt(p):
        chosen[p] = choose(p)
        start(chosen.at[p], pkv_all.at[mine_r], send.at[6], recv_pkv, "resp", p)

    others(resps, mine_r, send_prompt)
    pkv_all[mine_r] = choose(mine_r)

    q_all[own_rows, :] = q_mine[:, own_cols]
    g_all[own_rows, :] = g_mine[:, own_cols]
    head_of = lax.broadcasted_iota(jnp.int32, (group, width), 1) // HD
    ones = (head_of == lax.broadcasted_iota(jnp.int32, (group, width), 0)).astype(HALF)
    side = lax.rem(me, 2)
    first = (lax.broadcasted_iota(jnp.int32, (group, 2 * rows), 1) // rows) == side

    def delta_for(p):
        cols = pl.ds(pl.multiple_of(p * width, width), width)
        prod = o_mine[:, cols].astype(WIDE) * g_mine[:, cols].astype(WIDE)
        high = prod.astype(HALF)
        low = (prod - high.astype(WIDE)).astype(HALF)
        d = dot(ones, high, NT) + dot(ones, low, NT)
        return jnp.where(first, jnp.concatenate([d, d], axis=1), 0.0)

    def send_delta(p):
        delta_send[p] = delta_for(p)
        start(delta_send.at[p], delta_all.at[me], send.at[7], recv_delta, "heads", p)

    others(heads, me, send_delta)
    delta_all[me] = delta_for(me)

    def rest(stage, carry):
        send_stage(stage)
        return carry

    lax.fori_loop(1, stages, rest, 0)

    dk_acc[...] = jnp.zeros_like(dk_acc)
    dv_acc[...] = jnp.zeros_like(dv_acc)
    dpk_acc[...] = jnp.zeros_like(dpk_acc)
    dpv_acc[...] = jnp.zeros_like(dpv_acc)
    landed(k_all.at[pl.ds(0, total_rows - rows)], recv_kv.at[0])
    landed(v_all.at[pl.ds(0, total_rows - rows)], recv_kv.at[1])
    landed(delta_all.at[pl.ds(0, heads - 1)], recv_delta)
    landed(pkv_all.at[pl.ds(0, resps - 1)], recv_pkv)
    prompt_len = resps * span
    kt[...] = k_all[...].T
    pkt[...] = pkv_all[:, 0:span, :].reshape(prompt_len, HD).T
    delta_rows = jnp.concatenate(
        [delta_all[2 * i] + delta_all[2 * i + 1] for i in range(heads // 2)], axis=1
    )
    live = (lax.broadcasted_iota(jnp.int32, (1, total_rows), 1) < length[0]).astype(WIDE)
    causal = lax.broadcasted_iota(jnp.int32, (row_block, row_block), 0) <= lax.broadcasted_iota(
        jnp.int32, (row_block, row_block), 1
    )

    def one_block(head_in_group, delta_head, block):
        cols = pl.ds(pl.multiple_of(head_in_group * HD, HD), HD)
        lo = block * row_block
        at = slice(lo, lo + row_block)
        keys = lo + row_block
        q = q_all[lo : lo + row_block, cols]
        g = g_all[lo : lo + row_block, cols]
        pk = pkv_all[:, 0:span, :].reshape(prompt_len, HD)
        pv = pkv_all[:, span : 2 * span, :].reshape(prompt_len, HD)
        score_p = dot(pk, q, NT)
        score_r = dot(k_all[0:keys, :], q, NT)
        diag = jnp.where(causal, score_r[lo:keys], -jnp.inf)
        score_r = diag if lo == 0 else jnp.concatenate([score_r[0:lo], diag], axis=0)
        peak = jnp.maximum(
            jnp.max(score_p, axis=0, keepdims=True), jnp.max(score_r, axis=0, keepdims=True)
        )
        e_p = jnp.exp2((score_p - peak) * (scale * LOG2E))
        e_r = jnp.exp2((score_r - peak) * (scale * LOG2E))
        total = jnp.sum(e_p, axis=0, keepdims=True) + jnp.sum(e_r, axis=0, keepdims=True)
        norm = live[:, at] / total
        prob_p = e_p * norm
        prob_r = e_r * norm
        d = delta_head[:, at]
        ds_p = (prob_p * (dot(pv, g, NT) - d)).astype(HALF)
        ds_r = (prob_r * (dot(v_all[0:keys, :], g, NT) - d)).astype(HALF)
        prob_p = prob_p.astype(HALF)
        prob_r = prob_r.astype(HALF)
        dpv_acc[...] += dot(prob_p, g, NN)
        dv_acc[0:keys, :] += dot(prob_r, g, NN)
        dpk_acc[...] += dot(ds_p, q, NN)
        dk_acc[0:keys, :] += dot(ds_r, q, NN)
        dq_t = dot(pkt[...], ds_p, NN) + dot(kt[:, 0:keys], ds_r, NN)
        dq_all[lo : lo + row_block, cols] = (dq_t * scale).T.astype(HALF)

    def arrive(stage):
        landed(q_all.at[pl.ds(0, total_rows - rows), pl.ds(0, stage_width)], recv_q.at[stage])
        landed(g_all.at[pl.ds(0, total_rows - rows), pl.ds(0, stage_width)], recv_g.at[stage])

    def work(stage):
        for sub in range(per_stage):
            head_in_group = stage * per_stage + sub
            pick_head = (
                lax.broadcasted_iota(jnp.int32, (group, total_rows), 0) == head_in_group
            ).astype(WIDE)
            delta_head = jnp.sum(delta_rows * pick_head, axis=0, keepdims=True)
            for block in range(total_rows // row_block):
                one_block(head_in_group, delta_head, block)

    def give_back(stage):
        src_cols = pl.ds(pl.multiple_of(stage * stage_width, stage_width), stage_width)
        dst_cols = pl.ds(pl.multiple_of(me * width + stage * stage_width, stage_width), stage_width)

        def give(p):
            part_rows = pl.ds(pl.multiple_of(p * rows, rows), rows)
            start(
                dq_all.at[part_rows, src_cols],
                dq_out.at[:, dst_cols],
                send.at[8],
                recv_dq,
                "heads",
                p,
            )

        others(heads, me, give)

    def visit(stage, carry):
        arrive(stage)

        @pl.when(stage == stages - 1)
        def _():
            def earlier(s, carry):
                give_back(s)
                return carry

            lax.fori_loop(0, stages - 1, earlier, 0)

        work(stage)
        return carry

    lax.fori_loop(0, stages, visit, 0)
    give_back(stages - 1)

    for a in range(resps):
        lo = a * span
        term_send[a] = jnp.concatenate(
            [dpk_acc[lo : lo + span, :] * scale, dpv_acc[lo : lo + span, :]], axis=0
        ).astype(HALF)
    others(
        resps,
        mine_r,
        lambda p: start(term_send.at[p], term_all.at[mine_r], send.at[9], recv_term, "resp", p),
    )
    dk_half[...] = (dk_acc[...] * scale).astype(HALF)
    dv_half[...] = dv_acc[...].astype(HALF)

    def give_own(p):
        part_rows = pl.ds(pl.multiple_of(p * rows, rows), rows)
        start(dk_half.at[part_rows, :], dkv_out.at[0, :, own_head], send.at[10], recv_dkv.at[0], "heads", p)
        start(dv_half.at[part_rows, :], dkv_out.at[1, :, own_head], send.at[11], recv_dkv.at[1], "heads", p)

    others(heads, me, give_own)
    put = [
        pltpu.make_async_copy(dq_all.at[own_rows, :], dq_out.at[:, own_cols], local.at[0]),
        pltpu.make_async_copy(dk_half.at[own_rows, :], dkv_out.at[0, :, own_head], local.at[1]),
        pltpu.make_async_copy(dv_half.at[own_rows, :], dkv_out.at[1, :, own_head], local.at[2]),
    ]
    for copy in put:
        copy.start()
    term_all[mine_r] = term_send[mine_r]
    landed(term_all.at[pl.ds(0, resps - 1)], recv_term)
    sums = [jnp.zeros((2 * span, HD), WIDE) for c in range(prompt_count)]
    for a in range(resps):
        w = weights(a)
        term = term_all[a].astype(WIDE)
        sums = [s + w[c] * term for c, s in enumerate(sums)]
    for b in range(prompts):
        pieces = []
        for kv in range(2):
            for c in range(prompt_count):
                lo = kv * span + b * own_tokens
                pieces.append(sums[c][lo : lo + own_tokens])
        dense[b] = jnp.concatenate(pieces, axis=0)
    dense_all[mine_p] = dense[mine_p]
    others(
        prompts,
        mine_p,
        lambda p: start(dense.at[p], dense_all.at[mine_p], send.at[12], recv_dense, "prompt", p),
    )
    landed(dense_all.at[pl.ds(0, prompts - 1)], recv_dense)
    result = dense_all[0]
    for b in range(1, prompts):
        result = result + dense_all[b]
    for kv in range(2):
        lo = kv * part
        dpkv_out[kv] = jnp.stack(
            [
                result[lo + c * own_tokens : lo + (c + 1) * own_tokens]
                for c in range(prompt_count)
            ],
            axis=1,
        ).astype(HALF)

    for copy in put:
        copy.wait()
    far = pl.ds(0, (heads - 1) * width)
    far_kv = pl.ds(0, (heads - 1) * HD)
    landed(dq_out.at[:, far], recv_dq)
    landed(dkv_out.at[0, :, far_kv], recv_dkv.at[0])
    landed(dkv_out.at[1, :, far_kv], recv_dkv.at[1])
    landed(id_all.at[pl.ds(0, resps - 1)], send.at[0])
    landed(quarter.at[pl.ds(0, prompts - 1)], send.at[1])
    landed(k_all.at[pl.ds(0, total_rows - rows)], send.at[2])
    landed(v_all.at[pl.ds(0, total_rows - rows)], send.at[3])
    landed(q_all.at[pl.ds(0, total_rows - rows)], send.at[4])
    landed(g_all.at[pl.ds(0, total_rows - rows)], send.at[5])
    landed(chosen.at[pl.ds(0, resps - 1)], send.at[6])
    landed(delta_all.at[pl.ds(0, heads - 1)], send.at[7])
    landed(dq_all.at[pl.ds(0, total_rows - rows)], send.at[8])
    landed(term_all.at[pl.ds(0, resps - 1)], send.at[9])
    landed(dk_half.at[pl.ds(0, total_rows - rows)], send.at[10])
    landed(dv_half.at[pl.ds(0, total_rows - rows)], send.at[11])
    landed(dense_all.at[pl.ds(0, prompts - 1)], send.at[12])


def on_device(
    mesh_sizes,
    queries,
    outputs,
    out_grads,
    resp_keys,
    resp_values,
    prompt_keys,
    prompt_values,
    prompt_of,
    lengths,
):
    heads, resps, prompts = mesh_sizes
    rows = queries.shape[1]
    kv_heads = resp_keys.shape[2] // HD
    group = queries.shape[2] // HD // kv_heads
    own_tokens, prompt_count = prompt_keys.shape[:2]
    total_rows = heads * rows
    stages = 4
    row_block = total_rows // 2
    span = own_tokens * prompts
    prompt_len = span * resps
    width = group * HD
    sizes = (heads, resps, prompts, group, rows, stages, row_block, own_tokens, prompt_count)

    both = 2 * own_tokens * prompt_count
    vmem = pltpu.VMEM
    dma = pltpu.SemaphoreType.DMA
    in_hbm = functools.partial(pltpu.with_memory_space_constraint, memory_space=pltpu.HBM)
    hbm = pl.BlockSpec(memory_space=pl.ANY)
    smem = pl.BlockSpec(memory_space=pltpu.SMEM)
    in_vmem = pl.BlockSpec(memory_space=pltpu.VMEM)
    dq, dkv, dpkv = pl.pallas_call(
        functools.partial(kernel, sizes),
        out_shape=(
            jax.ShapeDtypeStruct((rows, queries.shape[2]), HALF),
            jax.ShapeDtypeStruct((2, rows, resp_keys.shape[2]), HALF),
            jax.ShapeDtypeStruct((2, own_tokens, prompt_count, HD), HALF),
        ),
        in_specs=[smem] * 2 + [hbm] * 7,
        out_specs=(hbm, hbm, in_vmem),
        scratch_shapes=[
            vmem((total_rows, width), HALF),
            vmem((total_rows, width), HALF),
            vmem((total_rows, HD), HALF),
            vmem((total_rows, HD), HALF),
            vmem((rows, queries.shape[2]), HALF),
            vmem((rows, queries.shape[2]), HALF),
            vmem((rows, queries.shape[2]), HALF),
            vmem((rows, resp_keys.shape[2]), HALF),
            vmem((rows, resp_keys.shape[2]), HALF),
            vmem((own_tokens, prompt_count, HD), HALF),
            vmem((own_tokens, prompt_count, HD), HALF),
            vmem((heads, group, 2 * rows), WIDE),
            vmem((heads, group, 2 * rows), WIDE),
            vmem((8, HD), WIDE),
            vmem((resps, 8, HD), WIDE),
            vmem((both, HD), HALF),
            vmem((prompts, both, HD), HALF),
            vmem((resps, 2 * span, HD), HALF),
            vmem((resps, 2 * span, HD), HALF),
            vmem((HD, total_rows), HALF),
            vmem((HD, prompt_len), HALF),
            vmem((total_rows, width), HALF),
            vmem((total_rows, HD), WIDE),
            vmem((total_rows, HD), WIDE),
            vmem((prompt_len, HD), WIDE),
            vmem((prompt_len, HD), WIDE),
            vmem((total_rows, HD), HALF),
            vmem((total_rows, HD), HALF),
            vmem((resps, 2 * span, HD), HALF),
            vmem((resps, 2 * span, HD), HALF),
            vmem((prompts, both, HD), WIDE),
            vmem((prompts, both, HD), WIDE),
            dma((13,)),
            dma,
            dma,
            dma,
            dma((2,)),
            dma,
            dma((stages,)),
            dma((stages,)),
            dma,
            dma((2,)),
            dma,
            dma,
            dma((7,)),
        ],
        compiler_params=pltpu.CompilerParams(
            collective_id=0, has_side_effects=True, vmem_limit_bytes=48 * 1024 * 1024
        ),
    )(
        prompt_of,
        lengths,
        in_hbm(queries[0]),
        in_hbm(outputs[0]),
        in_hbm(out_grads[0]),
        in_hbm(resp_keys[0]),
        in_hbm(resp_values[0]),
        in_hbm(prompt_keys),
        in_hbm(prompt_values),
    )
    return dq[None], dkv[0][None], dkv[1][None], dpkv[0], dpkv[1]


def solution(mesh):
    sizes = (mesh.shape["heads"], mesh.shape["resp"], mesh.shape["prompt"])
    return jax.shard_map(
        functools.partial(on_device, sizes),
        mesh=mesh,
        in_specs=(
            P(("resp", "prompt"), "heads", None),
            P(("resp", "prompt"), "heads", None),
            P(("resp", "prompt"), "heads", None),
            P(("resp", "prompt"), "heads", None),
            P(("resp", "prompt"), "heads", None),
            P(("resp", "prompt"), None, "heads"),
            P(("resp", "prompt"), None, "heads"),
            P(("resp", "prompt")),
            P(("resp", "prompt")),
        ),
        out_specs=(
            P(("resp", "prompt"), "heads", None),
            P(("resp", "prompt"), "heads", None),
            P(("resp", "prompt"), "heads", None),
            P(("resp", "prompt"), None, "heads"),
            P(("resp", "prompt"), None, "heads"),
        ),
        check_vma=False,
    )
```

```python
import functools

import jax
import jax.numpy as jnp
from jax import lax
from jax.experimental import pallas as pl
from jax.experimental.pallas import tpu as pltpu
from jax.sharding import PartitionSpec as P

HD = 128
LOG2E = 1.4426950408889634
WIDE = jnp.float32
HALF = jnp.bfloat16
NT = (((1,), (1,)), ((), ()))
NN = (((1,), (0,)), ((), ()))


def dot(a, b, dims):
    return lax.dot_general(a, b, dims, preferred_element_type=WIDE)


def kernel(
    sizes,
    prompt_id,
    length,
    q_in,
    o_in,
    g_in,
    k_in,
    v_in,
    pk_in,
    pv_in,
    dq_out,
    dkv_out,
    dpkv_out,
    qg_mine,
    o_mine,
    kv_mine,
    p_mine,
    qg_all,
    qg_far,
    kv_all,
    delta_send,
    delta_all,
    delta_far,
    id_send,
    id_all,
    packed,
    quarter,
    chosen,
    pkv_all,
    kt,
    pkt,
    dq_all,
    dq_far,
    dkv_acc,
    dp_acc,
    dkv_half,
    dkv_land,
    term_send,
    term_all,
    dense,
    dense_all,
    send,
    recv_id,
    recv_quarter,
    recv_pkv,
    recv_kv,
    recv_delta,
    recv_delta_far,
    recv_qg,
    recv_qg_far,
    recv_dq,
    recv_dq_far,
    recv_dkv,
    recv_term,
    recv_dense,
    local,
):
    heads, resps, prompts, group, rows, stages, own_tokens, prompt_count = sizes
    chips = heads // 2
    me = lax.axis_index("heads")
    chip, core = me // 2, lax.rem(me, 2)
    sibling = me + 1 - 2 * core
    far = lax.rem(me + chips, heads)
    far_chip = far // 2
    far_sibling = lax.rem(sibling + chips, heads)
    mine_r = lax.axis_index("resp")
    mine_p = lax.axis_index("prompt")
    chip_rows = 2 * rows
    total_rows = heads * rows
    width = group * HD
    per_stage = group // stages
    stage_width = per_stage * HD
    span = own_tokens * prompts
    prompt_len = resps * span
    part = prompt_count * own_tokens
    near = [
        (offset, side) for offset in range(1, chips) if 2 * offset != chips for side in (0, 1)
    ]
    n_near = len(near) + 1
    scale = HD**-0.5

    def start(src, dst, send_sem, recv_sem, axis, index):
        device = index if axis is None else {axis: index}
        pltpu.make_async_remote_copy(
            src_ref=src,
            dst_ref=dst,
            send_sem=send_sem,
            recv_sem=recv_sem,
            device_id=device,
            device_id_type=pl.DeviceIdType.MESH,
        ).start()

    def landed(ref, sem):
        pltpu.make_async_copy(ref, ref, sem).wait()

    def others(count, own, body):
        def step(i, carry):
            body(lax.rem(own + i, count))
            return carry

        lax.fori_loop(1, count, step, 0)

    def neighbours(body):
        for offset, side in near:
            body(lax.rem(chip + offset, chips) * 2 + side)
        body(sibling)

    def span_of(index, size):
        return pl.ds(pl.multiple_of(index * size, size), size)

    loads = [
        pltpu.make_async_copy(src, dst, local.at[n])
        for n, (src, dst) in enumerate(
            (
                (pk_in, p_mine.at[0]),
                (pv_in, p_mine.at[1]),
                (k_in, kv_mine.at[0]),
                (v_in, kv_mine.at[1]),
                (q_in, qg_mine.at[0]),
                (g_in, qg_mine.at[1]),
                (o_in, o_mine),
            )
        )
    ]
    for copy in loads:
        copy.start()
    own_rows = span_of(me, rows)
    side_rows = span_of(core, rows)

    delta_all[...] = jnp.zeros_like(delta_all)
    dkv_land[...] = jnp.zeros_like(dkv_land)
    barrier = pltpu.get_barrier_semaphore()
    for axis, count, own in (("heads", heads, me), ("resp", resps, mine_r), ("prompt", prompts, mine_p)):

        def greet(peer, axis=axis):
            pl.semaphore_signal(
                barrier, inc=1, device_id={axis: peer}, device_id_type=pl.DeviceIdType.MESH
            )

        others(count, own, greet)
    others(
        prompts,
        mine_p,
        lambda p: pl.semaphore_signal(
            barrier,
            inc=1,
            device_id={"heads": far, "prompt": p},
            device_id_type=pl.DeviceIdType.MESH,
        ),
    )
    for copy in loads[:2]:
        copy.wait()
    id_tile = jnp.full((8, HD), prompt_id[0], jnp.int32).astype(WIDE)
    id_send[...] = id_tile
    id_all[mine_r] = id_tile
    mine_k = p_mine[0].astype(WIDE)
    mine_v = p_mine[1].astype(WIDE)
    packed[...] = jnp.concatenate(
        [mine_k[:, c, :] for c in range(prompt_count)]
        + [mine_v[:, c, :] for c in range(prompt_count)],
        axis=0,
    ).astype(HALF)
    quarter[0, mine_p] = packed[...]
    for copy in loads[2:]:
        copy.wait()
    pl.semaphore_wait(barrier, heads + resps + 2 * prompts - 4)

    others(resps, mine_r, lambda p: start(id_send, id_all.at[mine_r], send.at[3], recv_id, "resp", p))
    others(
        prompts,
        mine_p,
        lambda p: start(packed, quarter.at[0, mine_p], send.at[0], recv_quarter.at[0], "prompt", p),
    )
    for offset in range(prompts):
        start(
            packed,
            quarter.at[1, mine_p],
            send.at[1],
            recv_quarter.at[1],
            None,
            {"heads": far, "prompt": lax.rem(mine_p + offset, prompts)},
        )

    def kv_cols(g, index):
        return span_of(index if g == 0 else lax.rem(index + chips, heads), HD)

    def send_kv(g):
        def body(p):
            def go():
                start(
                    kv_mine.at[:, :, kv_cols(g, p)],
                    kv_all.at[g, :, own_rows, :],
                    send.at[4 + g],
                    recv_kv.at[g],
                    "heads",
                    p,
                )

            if g == 0:
                go()
            else:
                pl.when(chip <= p // 2)(go)

        others(heads, me, body)
        kv_all[g, :, own_rows, :] = kv_mine[:, :, kv_cols(g, me)]

    send_kv(0)

    def send_stage(stage):
        to = span_of(stage, stage_width)

        def body(p):
            cols = pl.ds(pl.multiple_of(p * width + stage * stage_width, stage_width), stage_width)
            start(
                qg_mine.at[:, :, cols],
                qg_all.at[:, own_rows, to],
                send.at[6],
                recv_qg.at[stage],
                "heads",
                p,
            )

        neighbours(body)

    qg_far[:, side_rows, :] = qg_mine[:, :, span_of(far, width)]
    qg_all[:, own_rows, :] = qg_mine[:, :, span_of(me, width)]

    def weights(index):
        return [(id_all[index] == float(c)).astype(WIDE)[0:1] for c in range(prompt_count)]

    def choose_and_send(g):
        landed(quarter.at[g, pl.ds(0, prompts - 1 + g)], recv_quarter.at[g])
        held = [quarter[g, b].astype(WIDE) for b in range(prompts)]

        def pick(kv, c):
            lo = kv * part + c * own_tokens
            return jnp.concatenate([h[lo : lo + own_tokens] for h in held], axis=0)

        by_prompt = [jnp.concatenate([pick(0, c), pick(1, c)], axis=0) for c in range(prompt_count)]

        def choose(p):
            w = weights(p)
            out = w[0] * by_prompt[0]
            for c in range(1, prompt_count):
                out = out + w[c] * by_prompt[c]
            return out.astype(HALF)

        for a in range(resps):
            chosen[g, a] = choose(a)
        others(
            resps,
            mine_r,
            lambda p: start(
                chosen.at[g, p], pkv_all.at[g, mine_r], send.at[8 + g], recv_pkv.at[g], "resp", p
            ),
        )
        pkv_all[g, mine_r] = chosen[g, mine_r]

    landed(id_all.at[pl.ds(0, resps - 1)], recv_id)
    choose_and_send(0)
    send_stage(0)
    start(
        qg_mine.at[:, :, span_of(far_sibling, width)],
        qg_far.at[:, side_rows, :],
        send.at[7],
        recv_qg_far,
        "heads",
        sibling,
    )
    choose_and_send(1)
    send_stage(1)

    head_of = lax.broadcasted_iota(jnp.int32, (group, width), 1) // HD
    ones = (head_of == lax.broadcasted_iota(jnp.int32, (group, width), 0)).astype(HALF)
    first = (lax.broadcasted_iota(jnp.int32, (group, chip_rows), 1) // rows) == core

    def delta_for(p):
        cols = slice(p * width, (p + 1) * width)
        prod = o_mine[:, cols].astype(WIDE) * qg_mine[1, :, cols].astype(WIDE)
        high = prod.astype(HALF)
        low = (prod - high.astype(WIDE)).astype(HALF)
        d = dot(ones, high, NT) + dot(ones, low, NT)
        return jnp.where(first, jnp.concatenate([d, d], axis=1), 0.0)

    for p in range(heads):
        delta_send[p] = delta_for(p)
    neighbours(
        lambda p: start(delta_send.at[p], delta_all.at[me], send.at[10], recv_delta, "heads", p)
    )
    start(delta_send.at[far_sibling], delta_far.at[core], send.at[11], recv_delta_far, "heads", sibling)
    delta_all[me] = delta_send[me]
    delta_far[core] = delta_send[far]

    send_kv(1)

    def rest(stage, carry):
        send_stage(stage)
        return carry

    lax.fori_loop(2, stages, rest, 0)

    dkv_acc[...] = jnp.zeros_like(dkv_acc)
    dp_acc[...] = jnp.zeros_like(dp_acc)
    live = (lax.broadcasted_iota(jnp.int32, (1, total_rows), 1) < length[0]).astype(WIDE)
    lanes = per_stage * chip_rows
    causal = lax.broadcasted_iota(jnp.int32, (chip_rows, lanes), 0) <= lax.rem(
        lax.broadcasted_iota(jnp.int32, (chip_rows, lanes), 1), chip_rows
    )

    def transposed(g):
        kt[g] = kv_all[g, 0].T
        pkt[g] = pkv_all[g, :, 0:span, :].reshape(prompt_len, HD).T

    def blocks(g, work):
        pk = pkv_all[g, :, 0:span, :].reshape(prompt_len, HD)
        pv = pkv_all[g, :, span : 2 * span, :].reshape(prompt_len, HD)
        probs_p, probs_r, dscores_p, dscores_r = [], [], [], []
        for k, q, grad, d in work:
            lo = k * chip_rows
            keys = lo + chip_rows
            score_p = dot(pk, q, NT)
            score_r = dot(kv_all[g, 0, 0:keys, :], q, NT)
            diag = jnp.where(causal, score_r[lo:keys], -jnp.inf)
            score_r = diag if lo == 0 else jnp.concatenate([score_r[0:lo], diag], axis=0)
            peak = jnp.maximum(
                jnp.max(score_p, axis=0, keepdims=True), jnp.max(score_r, axis=0, keepdims=True)
            )
            e_p = jnp.exp2((score_p - peak) * (scale * LOG2E))
            e_r = jnp.exp2((score_r - peak) * (scale * LOG2E))
            total = jnp.sum(e_p, axis=0, keepdims=True) + jnp.sum(e_r, axis=0, keepdims=True)
            norm = jnp.concatenate([live[:, lo:keys]] * per_stage, axis=1) / total
            prob_p = e_p * norm
            prob_r = e_r * norm
            dscores_p.append((prob_p * (dot(pv, grad, NT) - d)).astype(HALF))
            dscores_r.append((prob_r * (dot(kv_all[g, 1, 0:keys, :], grad, NT) - d)).astype(HALF))
            probs_p.append(prob_p.astype(HALF))
            probs_r.append(prob_r.astype(HALF))
        every_q = jnp.concatenate([w[1] for w in work], axis=0)
        every_grad = jnp.concatenate([w[2] for w in work], axis=0)
        dp_acc[g, 1] += dot(jnp.concatenate(probs_p, axis=1), every_grad, NN)
        dp_acc[g, 0] += dot(jnp.concatenate(dscores_p, axis=1), every_q, NN)
        dqs = []
        for n, (k, q, grad, d) in enumerate(work):
            keys = (k + 1) * chip_rows
            dkv_acc[g, 1, 0:keys, :] += dot(probs_r[n], grad, NN)
            dkv_acc[g, 0, 0:keys, :] += dot(dscores_r[n], q, NN)
            dq_t = dot(pkt[g], dscores_p[n], NN) + dot(kt[g, :, 0:keys], dscores_r[n], NN)
            dqs.append((dq_t * scale).T.astype(HALF))
        return dqs

    def head_cols(stage, sub):
        return span_of(stage * per_stage + sub, HD)

    def delta_of(table, stage, lo):
        size = table.shape[1]
        out = []
        for sub in range(per_stage):
            mask = (
                lax.broadcasted_iota(jnp.int32, (group, size), 0) == stage * per_stage + sub
            ).astype(WIDE)
            out.append(jnp.sum(table * mask, axis=0, keepdims=True)[:, lo : lo + chip_rows])
        return jnp.concatenate(out, axis=1)

    def stacked(ref, kind, at, stage):
        return jnp.concatenate(
            [ref[kind, at, head_cols(stage, sub)] for sub in range(per_stage)], axis=0
        )

    def far_work():
        table = delta_far[0] + delta_far[1]
        every = slice(0, chip_rows)

        def visit(pair, carry):
            for k in range(chips):

                @pl.when(chip == k)
                def _(k=k):
                    both = [2 * pair, 2 * pair + 1]
                    dqs = blocks(
                        1,
                        [
                            (
                                k,
                                stacked(qg_far, 0, every, stage),
                                stacked(qg_far, 1, every, stage),
                                delta_of(table, stage, 0),
                            )
                            for stage in both
                        ],
                    )
                    for stage, dq in zip(both, dqs):
                        for sub in range(per_stage):
                            dq_far[:, head_cols(stage, sub)] = dq[
                                sub * chip_rows : (sub + 1) * chip_rows
                            ]

            return carry

        lax.fori_loop(0, stages // 2, visit, 0)

    def give_dkv(g):
        dkv_half[g, 0] = (dkv_acc[g, 0] * scale).astype(HALF)
        dkv_half[g, 1] = dkv_acc[g, 1].astype(HALF)
        cols = kv_cols(g, me)

        def body(p):
            def go():
                start(
                    dkv_half.at[g, :, span_of(p, rows), :],
                    dkv_land.at[g, :, :, cols],
                    send.at[12 + g],
                    recv_dkv.at[g],
                    "heads",
                    p,
                )

            if g == 0:
                go()
            else:
                pl.when(p // 2 <= chip)(go)

        others(heads, me, body)
        dkv_land[g, :, :, cols] = dkv_half[g, :, own_rows, :]

    def send_terms(g):
        for a in range(resps):
            lo = a * span
            term_send[g, a] = jnp.concatenate(
                [dp_acc[g, 0, lo : lo + span, :] * scale, dp_acc[g, 1, lo : lo + span, :]], axis=0
            ).astype(HALF)
        others(
            resps,
            mine_r,
            lambda p: start(
                term_send.at[g, p], term_all.at[g, mine_r], send.at[14 + g], recv_term.at[g], "resp", p
            ),
        )
        term_all[g, mine_r] = term_send[g, mine_r]

    def send_dense(g):
        landed(term_all.at[g, pl.ds(0, resps - 1)], recv_term.at[g])

        def add(a, sums):
            w = weights(a)
            term = term_all[g, a].astype(WIDE)
            return tuple(s + w[c] * term for c, s in enumerate(sums))

        sums = lax.fori_loop(
            0, resps, add, tuple(jnp.zeros((2 * span, HD), WIDE) for c in range(prompt_count))
        )
        for b in range(prompts):
            pieces = []
            for kv in range(2):
                for c in range(prompt_count):
                    lo = kv * span + b * own_tokens
                    pieces.append(sums[c][lo : lo + own_tokens])
            dense[g, b] = jnp.concatenate(pieces, axis=0)
        if g == 0:
            dense_all[0, mine_p] = dense[0, mine_p]
        for offset in range(1 - g, prompts):
            p = lax.rem(mine_p + offset, prompts)
            start(
                dense.at[g, p],
                dense_all.at[g, mine_p],
                send.at[16 + g],
                recv_dense.at[g],
                None,
                {"heads": me if g == 0 else far, "prompt": p},
            )

    landed(kv_all.at[0, :, pl.ds(0, total_rows - rows), :], recv_kv.at[0])
    landed(delta_all.at[pl.ds(0, n_near)], recv_delta)
    landed(pkv_all.at[0, pl.ds(0, resps - 1)], recv_pkv.at[0])
    transposed(0)
    delta_rows = jnp.concatenate(
        [delta_all[2 * k] + delta_all[2 * k + 1] for k in range(chips)], axis=1
    )

    def give_back(stage):
        src_cols = span_of(stage, stage_width)
        dst_cols = pl.ds(pl.multiple_of(me * width + stage * stage_width, stage_width), stage_width)
        neighbours(
            lambda p: start(
                dq_all.at[span_of(p, rows), src_cols],
                dq_out.at[:, dst_cols],
                send.at[18],
                recv_dq,
                "heads",
                p,
            )
        )

    def visit(stage, carry):
        landed(qg_all.at[:, pl.ds(0, n_near * rows), pl.ds(0, stage_width)], recv_qg.at[stage])
        for away in range(chips):

            @pl.when(far_chip == away)
            def _(away=away):
                chosen_chips = [k for k in range(chips) if k != away]
                places = [slice(k * chip_rows, (k + 1) * chip_rows) for k in chosen_chips]
                dqs = blocks(
                    0,
                    [
                        (
                            k,
                            stacked(qg_all, 0, at, stage),
                            stacked(qg_all, 1, at, stage),
                            delta_of(delta_rows, stage, k * chip_rows),
                        )
                        for k, at in zip(chosen_chips, places)
                    ],
                )
                for at, dq in zip(places, dqs):
                    for sub in range(per_stage):
                        dq_all[at, head_cols(stage, sub)] = dq[
                            sub * chip_rows : (sub + 1) * chip_rows
                        ]

        @pl.when(stage < stages - 1)
        def _():
            give_back(stage)

        @pl.when(stage == 0)
        def _():
            for k in range(chips):

                @pl.when(chip == k)
                def _(k=k):
                    landed(kv_all.at[1, :, pl.ds(0, (2 * k + 1) * rows), :], recv_kv.at[1])

            landed(delta_far.at[0], recv_delta_far)
            landed(qg_far.at[:, pl.ds(0, rows), :], recv_qg_far)
            landed(pkv_all.at[1, pl.ds(0, resps - 1)], recv_pkv.at[1])
            transposed(1)
            far_work()
            start(
                dq_far.at[span_of(1 - core, rows), :],
                dq_out.at[:, span_of(far, width)],
                send.at[19],
                recv_dq_far,
                "heads",
                sibling,
            )
            send_terms(1)
            give_dkv(1)

        return carry

    lax.fori_loop(0, stages, visit, 0)

    send_terms(0)
    give_back(stages - 1)
    give_dkv(0)
    put = [
        pltpu.make_async_copy(
            dq_all.at[own_rows, :], dq_out.at[:, span_of(me, width)], local.at[0]
        ),
        pltpu.make_async_copy(
            dq_far.at[side_rows, :], dq_out.at[:, span_of(far, width)], local.at[1]
        ),
    ]
    for copy in put:
        copy.start()
    send_dense(1)
    send_dense(0)
    for g in range(2):
        landed(dense_all.at[g, pl.ds(0, prompts - 1 + g)], recv_dense.at[g])
    result = dense_all[0, 0]
    for b in range(1, prompts):
        result = result + dense_all[0, b]
    for b in range(prompts):
        result = result + dense_all[1, b]
    for kv in range(2):
        lo = kv * part
        dpkv_out[kv] = jnp.stack(
            [
                result[lo + c * own_tokens : lo + (c + 1) * own_tokens]
                for c in range(prompt_count)
            ],
            axis=1,
        ).astype(HALF)

    landed(dkv_land.at[0, :, :, pl.ds(0, (heads - 1) * HD)], recv_dkv.at[0])
    for k in range(chips):

        @pl.when(chip == k)
        def _(k=k):
            from_later = 2 * (chips - k) - 1
            landed(dkv_land.at[1, :, :, pl.ds(0, from_later * HD)], recv_dkv.at[1])
            landed(kv_all.at[1, :, pl.ds(0, from_later * rows), :], send.at[5])
            landed(kv_all.at[1, :, pl.ds(0, (2 * k + 1) * rows), :], send.at[13])

    for kv in range(2):
        dkv_out[kv] = (dkv_land[0, kv].astype(WIDE) + dkv_land[1, kv].astype(WIDE)).astype(HALF)

    for copy in put:
        copy.wait()
    landed(dq_out.at[:, pl.ds(0, n_near * width)], recv_dq)
    landed(dq_out.at[:, pl.ds(0, width)], recv_dq_far)
    for g in range(2):
        landed(quarter.at[g, pl.ds(0, prompts - 1 + g)], send.at[g])
        landed(chosen.at[g, pl.ds(0, resps - 1)], send.at[8 + g])
        landed(term_all.at[g, pl.ds(0, resps - 1)], send.at[14 + g])
        landed(dense_all.at[g, pl.ds(0, prompts - 1 + g)], send.at[16 + g])
    landed(id_all.at[pl.ds(0, resps - 1)], send.at[3])
    landed(kv_all.at[0, :, pl.ds(0, total_rows - rows), :], send.at[4])
    landed(qg_all.at[:, pl.ds(0, n_near * rows), :], send.at[6])
    landed(qg_far.at[:, pl.ds(0, rows), :], send.at[7])
    landed(delta_all.at[pl.ds(0, n_near)], send.at[10])
    landed(delta_far.at[0], send.at[11])
    landed(dkv_half.at[0, :, pl.ds(0, total_rows - rows), :], send.at[12])
    landed(dq_all.at[pl.ds(0, n_near * rows), :], send.at[18])
    landed(dq_far.at[pl.ds(0, rows), :], send.at[19])


def on_device(
    mesh_sizes,
    queries,
    outputs,
    out_grads,
    resp_keys,
    resp_values,
    prompt_keys,
    prompt_values,
    prompt_of,
    lengths,
):
    heads, resps, prompts = mesh_sizes
    rows = queries.shape[1]
    kv_heads = resp_keys.shape[2] // HD
    group = queries.shape[2] // HD // kv_heads
    own_tokens, prompt_count = prompt_keys.shape[:2]
    total_rows = heads * rows
    stages = 4
    span = own_tokens * prompts
    prompt_len = span * resps
    width = group * HD
    sizes = (heads, resps, prompts, group, rows, stages, own_tokens, prompt_count)
    columns = queries.shape[2]
    kv_columns = resp_keys.shape[2]
    chip_rows = 2 * rows
    both = 2 * own_tokens * prompt_count
    vmem = pltpu.VMEM
    dma = pltpu.SemaphoreType.DMA
    in_hbm = functools.partial(pltpu.with_memory_space_constraint, memory_space=pltpu.HBM)
    hbm = pl.BlockSpec(memory_space=pl.ANY)
    smem = pl.BlockSpec(memory_space=pltpu.SMEM)
    in_vmem = pl.BlockSpec(memory_space=pltpu.VMEM)
    dq, dkv, dpkv = pl.pallas_call(
        functools.partial(kernel, sizes),
        out_shape=(
            jax.ShapeDtypeStruct((rows, queries.shape[2]), HALF),
            jax.ShapeDtypeStruct((2, rows, resp_keys.shape[2]), HALF),
            jax.ShapeDtypeStruct((2, own_tokens, prompt_count, HD), HALF),
        ),
        in_specs=[smem] * 2 + [hbm] * 7,
        out_specs=(hbm, in_vmem, in_vmem),
        scratch_shapes=[
            vmem((2, rows, columns), HALF),
            vmem((rows, columns), HALF),
            vmem((2, rows, kv_columns), HALF),
            vmem((2, own_tokens, prompt_count, HD), HALF),
            vmem((2, total_rows, width), HALF),
            vmem((2, chip_rows, width), HALF),
            vmem((2, 2, total_rows, HD), HALF),
            vmem((heads, group, chip_rows), WIDE),
            vmem((heads, group, chip_rows), WIDE),
            vmem((2, group, chip_rows), WIDE),
            vmem((8, HD), WIDE),
            vmem((resps, 8, HD), WIDE),
            vmem((both, HD), HALF),
            vmem((2, prompts, both, HD), HALF),
            vmem((2, resps, 2 * span, HD), HALF),
            vmem((2, resps, 2 * span, HD), HALF),
            vmem((2, HD, total_rows), HALF),
            vmem((2, HD, prompt_len), HALF),
            vmem((total_rows, width), HALF),
            vmem((chip_rows, width), HALF),
            vmem((2, 2, total_rows, HD), WIDE),
            vmem((2, 2, prompt_len, HD), WIDE),
            vmem((2, 2, total_rows, HD), HALF),
            vmem((2, 2, rows, kv_columns), HALF),
            vmem((2, resps, 2 * span, HD), HALF),
            vmem((2, resps, 2 * span, HD), HALF),
            vmem((2, prompts, both, HD), WIDE),
            vmem((2, prompts, both, HD), WIDE),
            dma((20,)),
            dma,
            dma((2,)),
            dma((2,)),
            dma((2,)),
            dma,
            dma,
            dma((stages,)),
            dma,
            dma,
            dma,
            dma((2,)),
            dma((2,)),
            dma((2,)),
            dma((7,)),
        ],
        compiler_params=pltpu.CompilerParams(
            collective_id=0, has_side_effects=True, vmem_limit_bytes=48 * 1024 * 1024
        ),
    )(
        prompt_of,
        lengths,
        in_hbm(queries[0]),
        in_hbm(outputs[0]),
        in_hbm(out_grads[0]),
        in_hbm(resp_keys[0]),
        in_hbm(resp_values[0]),
        in_hbm(prompt_keys),
        in_hbm(prompt_values),
    )
    return dq[None], dkv[0][None], dkv[1][None], dpkv[0], dpkv[1]


def solution(mesh):
    sizes = (mesh.shape["heads"], mesh.shape["resp"], mesh.shape["prompt"])
    return jax.shard_map(
        functools.partial(on_device, sizes),
        mesh=mesh,
        in_specs=(
            P(("resp", "prompt"), "heads", None),
            P(("resp", "prompt"), "heads", None),
            P(("resp", "prompt"), "heads", None),
            P(("resp", "prompt"), "heads", None),
            P(("resp", "prompt"), "heads", None),
            P(("resp", "prompt"), None, "heads"),
            P(("resp", "prompt"), None, "heads"),
            P(("resp", "prompt")),
            P(("resp", "prompt")),
        ),
        out_specs=(
            P(("resp", "prompt"), "heads", None),
            P(("resp", "prompt"), "heads", None),
            P(("resp", "prompt"), "heads", None),
            P(("resp", "prompt"), None, "heads"),
            P(("resp", "prompt"), None, "heads"),
        ),
        check_vma=False,
    )
```

```python
import functools

import jax
import jax.numpy as jnp
from jax import lax
from jax.experimental import pallas as pl
from jax.experimental.pallas import tpu as pltpu
from jax.sharding import PartitionSpec as P

HD = 128
LOG2E = 1.4426950408889634
WIDE = jnp.float32
HALF = jnp.bfloat16
NT = (((1,), (1,)), ((), ()))
NN = (((1,), (0,)), ((), ()))


def dot(a, b, dims):
    return lax.dot_general(a, b, dims, preferred_element_type=WIDE)


def kernel(
    sizes,
    prompt_id,
    length,
    q_in,
    o_in,
    g_in,
    k_in,
    v_in,
    pk_in,
    pv_in,
    dq_out,
    dkv_out,
    dpkv_out,
    q_all,
    g_all,
    k_all,
    v_all,
    q_mine,
    o_mine,
    g_mine,
    k_mine,
    v_mine,
    pk_mine,
    pv_mine,
    delta_send,
    delta_all,
    id_send,
    id_all,
    pkv_send,
    quarter,
    chosen,
    pkv_all,
    kt,
    pkt,
    dq_all,
    dk_acc,
    dv_acc,
    dpk_acc,
    dpv_acc,
    dk_half,
    dv_half,
    term_send,
    term_all,
    dense,
    dense_all,
    send,
    recv_id,
    recv_quarter,
    recv_pkv,
    recv_kv,
    recv_delta,
    recv_q,
    recv_g,
    recv_dq,
    recv_dkv,
    recv_term,
    recv_dense,
    local,
):
    heads, resps, prompts, group, rows, stages, row_block, own_tokens, prompt_count = sizes
    me = lax.axis_index("heads")
    mine_r = lax.axis_index("resp")
    mine_p = lax.axis_index("prompt")
    total_rows = heads * rows
    width = group * HD
    per_stage = group // stages
    stage_width = per_stage * HD
    span = own_tokens * prompts
    scale = HD**-0.5

    def start(src, dst, send_sem, recv_sem, axis, index):
        pltpu.make_async_remote_copy(
            src_ref=src,
            dst_ref=dst,
            send_sem=send_sem,
            recv_sem=recv_sem,
            device_id={axis: index},
            device_id_type=pl.DeviceIdType.MESH,
        ).start()

    def landed(ref, sem):
        pltpu.make_async_copy(ref, ref, sem).wait()

    def others(count, own, body):
        def step(i, carry):
            body(lax.rem(own + i, count))
            return carry

        lax.fori_loop(1, count, step, 0)

    loads = [
        pltpu.make_async_copy(src, dst, local.at[n])
        for n, (src, dst) in enumerate(
            (
                (pk_in, pk_mine),
                (pv_in, pv_mine),
                (k_in, k_mine),
                (v_in, v_mine),
                (q_in, q_mine),
                (g_in, g_mine),
                (o_in, o_mine),
            )
        )
    ]
    for copy in loads:
        copy.start()
    own_cols = pl.ds(pl.multiple_of(me * width, width), width)
    own_rows = pl.ds(pl.multiple_of(me * rows, rows), rows)
    own_head = pl.ds(pl.multiple_of(me * HD, HD), HD)

    barrier = pltpu.get_barrier_semaphore()
    for axis, count, own in (("heads", heads, me), ("resp", resps, mine_r), ("prompt", prompts, mine_p)):

        def greet(peer, axis=axis):
            pl.semaphore_signal(
                barrier, inc=1, device_id={axis: peer}, device_id_type=pl.DeviceIdType.MESH
            )

        others(count, own, greet)
    for copy in loads[:2]:
        copy.wait()
    id_tile = jnp.full((8, HD), prompt_id[0], jnp.int32).astype(WIDE)
    id_send[...] = id_tile
    id_all[mine_r] = id_tile
    mine_k = pk_mine[...].astype(WIDE)
    mine_v = pv_mine[...].astype(WIDE)
    pkv_send[...] = jnp.concatenate(
        [mine_k[:, c, :] for c in range(prompt_count)]
        + [mine_v[:, c, :] for c in range(prompt_count)],
        axis=0,
    ).astype(HALF)
    quarter[mine_p] = pkv_send[...]
    for copy in loads[2:]:
        copy.wait()
    pl.semaphore_wait(barrier, heads + resps + prompts - 3)

    others(resps, mine_r, lambda p: start(id_send, id_all.at[mine_r], send.at[0], recv_id, "resp", p))
    others(
        prompts,
        mine_p,
        lambda p: start(pkv_send, quarter.at[mine_p], send.at[1], recv_quarter, "prompt", p),
    )

    def send_kv(p):
        cols = pl.ds(pl.multiple_of(p * HD, HD), HD)
        start(k_mine.at[:, cols], k_all.at[own_rows, :], send.at[2], recv_kv.at[0], "heads", p)
        start(v_mine.at[:, cols], v_all.at[own_rows, :], send.at[3], recv_kv.at[1], "heads", p)

    others(heads, me, send_kv)
    k_all[own_rows, :] = k_mine[:, own_head]
    v_all[own_rows, :] = v_mine[:, own_head]

    def send_stage(stage):
        to = pl.ds(pl.multiple_of(stage * stage_width, stage_width), stage_width)

        def body(p):
            cols = pl.ds(pl.multiple_of(p * width + stage * stage_width, stage_width), stage_width)
            start(q_mine.at[:, cols], q_all.at[own_rows, to], send.at[4], recv_q.at[stage], "heads", p)
            start(g_mine.at[:, cols], g_all.at[own_rows, to], send.at[5], recv_g.at[stage], "heads", p)

        others(heads, me, body)

    send_stage(0)

    landed(quarter.at[pl.ds(0, prompts - 1)], recv_quarter)
    landed(id_all.at[pl.ds(0, resps - 1)], recv_id)
    held = [quarter[b].astype(WIDE) for b in range(prompts)]
    part = prompt_count * own_tokens

    def pick(kv, c):
        lo = kv * part + c * own_tokens
        return jnp.concatenate([h[lo : lo + own_tokens] for h in held], axis=0)

    by_prompt = [jnp.concatenate([pick(0, c), pick(1, c)], axis=0) for c in range(prompt_count)]

    def weights(index):
        return [(id_all[index] == float(c)).astype(WIDE)[0:1] for c in range(prompt_count)]

    def choose(p):
        w = weights(p)
        out = w[0] * by_prompt[0]
        for c in range(1, prompt_count):
            out = out + w[c] * by_prompt[c]
        return out.astype(HALF)

    def send_prompt(p):
        chosen[p] = choose(p)
        start(chosen.at[p], pkv_all.at[mine_r], send.at[6], recv_pkv, "resp", p)

    others(resps, mine_r, send_prompt)
    pkv_all[mine_r] = choose(mine_r)

    q_all[own_rows, :] = q_mine[:, own_cols]
    g_all[own_rows, :] = g_mine[:, own_cols]
    head_of = lax.broadcasted_iota(jnp.int32, (group, width), 1) // HD
    ones = (head_of == lax.broadcasted_iota(jnp.int32, (group, width), 0)).astype(HALF)
    side = lax.rem(me, 2)
    first = (lax.broadcasted_iota(jnp.int32, (group, 2 * rows), 1) // rows) == side

    def delta_for(p):
        cols = pl.ds(pl.multiple_of(p * width, width), width)
        prod = o_mine[:, cols].astype(WIDE) * g_mine[:, cols].astype(WIDE)
        high = prod.astype(HALF)
        low = (prod - high.astype(WIDE)).astype(HALF)
        d = dot(ones, high, NT) + dot(ones, low, NT)
        return jnp.where(first, jnp.concatenate([d, d], axis=1), 0.0)

    def send_delta(p):
        delta_send[p] = delta_for(p)
        start(delta_send.at[p], delta_all.at[me], send.at[7], recv_delta, "heads", p)

    others(heads, me, send_delta)
    delta_all[me] = delta_for(me)

    def rest(stage, carry):
        send_stage(stage)
        return carry

    lax.fori_loop(1, stages, rest, 0)

    dk_acc[...] = jnp.zeros_like(dk_acc)
    dv_acc[...] = jnp.zeros_like(dv_acc)
    dpk_acc[...] = jnp.zeros_like(dpk_acc)
    dpv_acc[...] = jnp.zeros_like(dpv_acc)
    landed(k_all.at[pl.ds(0, total_rows - rows)], recv_kv.at[0])
    landed(v_all.at[pl.ds(0, total_rows - rows)], recv_kv.at[1])
    landed(delta_all.at[pl.ds(0, heads - 1)], recv_delta)
    landed(pkv_all.at[pl.ds(0, resps - 1)], recv_pkv)
    prompt_len = resps * span
    kt[...] = k_all[...].T
    pkt[...] = pkv_all[:, 0:span, :].reshape(prompt_len, HD).T
    delta_rows = jnp.concatenate(
        [delta_all[2 * i] + delta_all[2 * i + 1] for i in range(heads // 2)], axis=1
    )
    live = (lax.broadcasted_iota(jnp.int32, (1, total_rows), 1) < length[0]).astype(WIDE)
    causal = lax.broadcasted_iota(jnp.int32, (row_block, row_block), 0) <= lax.broadcasted_iota(
        jnp.int32, (row_block, row_block), 1
    )

    def one_block(head_in_group, delta_head, block):
        cols = pl.ds(pl.multiple_of(head_in_group * HD, HD), HD)
        lo = block * row_block
        at = slice(lo, lo + row_block)
        keys = lo + row_block
        q = q_all[lo : lo + row_block, cols]
        g = g_all[lo : lo + row_block, cols]
        pk = pkv_all[:, 0:span, :].reshape(prompt_len, HD)
        pv = pkv_all[:, span : 2 * span, :].reshape(prompt_len, HD)
        score_p = dot(pk, q, NT)
        score_r = dot(k_all[0:keys, :], q, NT)
        diag = jnp.where(causal, score_r[lo:keys], -jnp.inf)
        score_r = diag if lo == 0 else jnp.concatenate([score_r[0:lo], diag], axis=0)
        peak = jnp.maximum(
            jnp.max(score_p, axis=0, keepdims=True), jnp.max(score_r, axis=0, keepdims=True)
        )
        e_p = jnp.exp2((score_p - peak) * (scale * LOG2E))
        e_r = jnp.exp2((score_r - peak) * (scale * LOG2E))
        total = jnp.sum(e_p, axis=0, keepdims=True) + jnp.sum(e_r, axis=0, keepdims=True)
        norm = live[:, at] / total
        prob_p = e_p * norm
        prob_r = e_r * norm
        d = delta_head[:, at]
        ds_p = (prob_p * (dot(pv, g, NT) - d)).astype(HALF)
        ds_r = (prob_r * (dot(v_all[0:keys, :], g, NT) - d)).astype(HALF)
        prob_p = prob_p.astype(HALF)
        prob_r = prob_r.astype(HALF)
        dpv_acc[...] += dot(prob_p, g, NN)
        dv_acc[0:keys, :] += dot(prob_r, g, NN)
        dpk_acc[...] += dot(ds_p, q, NN)
        dk_acc[0:keys, :] += dot(ds_r, q, NN)
        dq_t = dot(pkt[...], ds_p, NN) + dot(kt[:, 0:keys], ds_r, NN)
        dq_all[lo : lo + row_block, cols] = (dq_t * scale).T.astype(HALF)

    def arrive(stage):
        landed(q_all.at[pl.ds(0, total_rows - rows), pl.ds(0, stage_width)], recv_q.at[stage])
        landed(g_all.at[pl.ds(0, total_rows - rows), pl.ds(0, stage_width)], recv_g.at[stage])

    def work(stage):
        for sub in range(per_stage):
            head_in_group = stage * per_stage + sub
            pick_head = (
                lax.broadcasted_iota(jnp.int32, (group, total_rows), 0) == head_in_group
            ).astype(WIDE)
            delta_head = jnp.sum(delta_rows * pick_head, axis=0, keepdims=True)
            for block in range(total_rows // row_block):
                one_block(head_in_group, delta_head, block)

    def give_back(stage):
        src_cols = pl.ds(pl.multiple_of(stage * stage_width, stage_width), stage_width)
        dst_cols = pl.ds(pl.multiple_of(me * width + stage * stage_width, stage_width), stage_width)

        def give(p):
            part_rows = pl.ds(pl.multiple_of(p * rows, rows), rows)
            start(
                dq_all.at[part_rows, src_cols],
                dq_out.at[:, dst_cols],
                send.at[8],
                recv_dq,
                "heads",
                p,
            )

        others(heads, me, give)

    def visit(stage, carry):
        arrive(stage)

        @pl.when(stage == stages - 1)
        def _():
            def earlier(s, carry):
                give_back(s)
                return carry

            lax.fori_loop(0, stages - 1, earlier, 0)

        work(stage)
        return carry

    lax.fori_loop(0, stages, visit, 0)
    give_back(stages - 1)

    dk_half[...] = (dk_acc[...] * scale).astype(HALF)
    dv_half[...] = dv_acc[...].astype(HALF)

    def give_own(p):
        part_rows = pl.ds(pl.multiple_of(p * rows, rows), rows)
        start(dk_half.at[part_rows, :], dkv_out.at[0, :, own_head], send.at[10], recv_dkv.at[0], "heads", p)
        start(dv_half.at[part_rows, :], dkv_out.at[1, :, own_head], send.at[11], recv_dkv.at[1], "heads", p)

    others(heads, me, give_own)
    for a in range(resps):
        lo = a * span
        term_send[a] = jnp.concatenate(
            [dpk_acc[lo : lo + span, :] * scale, dpv_acc[lo : lo + span, :]], axis=0
        ).astype(HALF)
    others(
        resps,
        mine_r,
        lambda p: start(term_send.at[p], term_all.at[mine_r], send.at[9], recv_term, "resp", p),
    )
    put = [
        pltpu.make_async_copy(dq_all.at[own_rows, :], dq_out.at[:, own_cols], local.at[0]),
        pltpu.make_async_copy(dk_half.at[own_rows, :], dkv_out.at[0, :, own_head], local.at[1]),
        pltpu.make_async_copy(dv_half.at[own_rows, :], dkv_out.at[1, :, own_head], local.at[2]),
    ]
    for copy in put:
        copy.start()
    term_all[mine_r] = term_send[mine_r]
    landed(term_all.at[pl.ds(0, resps - 1)], recv_term)
    sums = [jnp.zeros((2 * span, HD), WIDE) for c in range(prompt_count)]
    for a in range(resps):
        w = weights(a)
        term = term_all[a].astype(WIDE)
        sums = [s + w[c] * term for c, s in enumerate(sums)]
    for b in range(prompts):
        pieces = []
        for kv in range(2):
            for c in range(prompt_count):
                lo = kv * span + b * own_tokens
                pieces.append(sums[c][lo : lo + own_tokens])
        dense[b] = jnp.concatenate(pieces, axis=0)
    dense_all[mine_p] = dense[mine_p]
    others(
        prompts,
        mine_p,
        lambda p: start(dense.at[p], dense_all.at[mine_p], send.at[12], recv_dense, "prompt", p),
    )
    landed(dense_all.at[pl.ds(0, prompts - 1)], recv_dense)
    result = dense_all[0]
    for b in range(1, prompts):
        result = result + dense_all[b]
    for kv in range(2):
        lo = kv * part
        dpkv_out[kv] = jnp.stack(
            [
                result[lo + c * own_tokens : lo + (c + 1) * own_tokens]
                for c in range(prompt_count)
            ],
            axis=1,
        ).astype(HALF)

    for copy in put:
        copy.wait()
    far = pl.ds(0, (heads - 1) * width)
    far_kv = pl.ds(0, (heads - 1) * HD)
    landed(dq_out.at[:, far], recv_dq)
    landed(dkv_out.at[0, :, far_kv], recv_dkv.at[0])
    landed(dkv_out.at[1, :, far_kv], recv_dkv.at[1])
    landed(id_all.at[pl.ds(0, resps - 1)], send.at[0])
    landed(quarter.at[pl.ds(0, prompts - 1)], send.at[1])
    landed(k_all.at[pl.ds(0, total_rows - rows)], send.at[2])
    landed(v_all.at[pl.ds(0, total_rows - rows)], send.at[3])
    landed(q_all.at[pl.ds(0, total_rows - rows)], send.at[4])
    landed(g_all.at[pl.ds(0, total_rows - rows)], send.at[5])
    landed(chosen.at[pl.ds(0, resps - 1)], send.at[6])
    landed(delta_all.at[pl.ds(0, heads - 1)], send.at[7])
    landed(dq_all.at[pl.ds(0, total_rows - rows)], send.at[8])
    landed(term_all.at[pl.ds(0, resps - 1)], send.at[9])
    landed(dk_half.at[pl.ds(0, total_rows - rows)], send.at[10])
    landed(dv_half.at[pl.ds(0, total_rows - rows)], send.at[11])
    landed(dense_all.at[pl.ds(0, prompts - 1)], send.at[12])


def on_device(
    mesh_sizes,
    queries,
    outputs,
    out_grads,
    resp_keys,
    resp_values,
    prompt_keys,
    prompt_values,
    prompt_of,
    lengths,
):
    heads, resps, prompts = mesh_sizes
    rows = queries.shape[1]
    kv_heads = resp_keys.shape[2] // HD
    group = queries.shape[2] // HD // kv_heads
    own_tokens, prompt_count = prompt_keys.shape[:2]
    total_rows = heads * rows
    stages = 4
    row_block = total_rows // 2
    span = own_tokens * prompts
    prompt_len = span * resps
    width = group * HD
    sizes = (heads, resps, prompts, group, rows, stages, row_block, own_tokens, prompt_count)

    both = 2 * own_tokens * prompt_count
    vmem = pltpu.VMEM
    dma = pltpu.SemaphoreType.DMA
    in_hbm = functools.partial(pltpu.with_memory_space_constraint, memory_space=pltpu.HBM)
    hbm = pl.BlockSpec(memory_space=pl.ANY)
    smem = pl.BlockSpec(memory_space=pltpu.SMEM)
    in_vmem = pl.BlockSpec(memory_space=pltpu.VMEM)
    dq, dkv, dpkv = pl.pallas_call(
        functools.partial(kernel, sizes),
        out_shape=(
            jax.ShapeDtypeStruct((rows, queries.shape[2]), HALF),
            jax.ShapeDtypeStruct((2, rows, resp_keys.shape[2]), HALF),
            jax.ShapeDtypeStruct((2, own_tokens, prompt_count, HD), HALF),
        ),
        in_specs=[smem] * 2 + [hbm] * 7,
        out_specs=(hbm, hbm, in_vmem),
        scratch_shapes=[
            vmem((total_rows, width), HALF),
            vmem((total_rows, width), HALF),
            vmem((total_rows, HD), HALF),
            vmem((total_rows, HD), HALF),
            vmem((rows, queries.shape[2]), HALF),
            vmem((rows, queries.shape[2]), HALF),
            vmem((rows, queries.shape[2]), HALF),
            vmem((rows, resp_keys.shape[2]), HALF),
            vmem((rows, resp_keys.shape[2]), HALF),
            vmem((own_tokens, prompt_count, HD), HALF),
            vmem((own_tokens, prompt_count, HD), HALF),
            vmem((heads, group, 2 * rows), WIDE),
            vmem((heads, group, 2 * rows), WIDE),
            vmem((8, HD), WIDE),
            vmem((resps, 8, HD), WIDE),
            vmem((both, HD), HALF),
            vmem((prompts, both, HD), HALF),
            vmem((resps, 2 * span, HD), HALF),
            vmem((resps, 2 * span, HD), HALF),
            vmem((HD, total_rows), HALF),
            vmem((HD, prompt_len), HALF),
            vmem((total_rows, width), HALF),
            vmem((total_rows, HD), WIDE),
            vmem((total_rows, HD), WIDE),
            vmem((prompt_len, HD), WIDE),
            vmem((prompt_len, HD), WIDE),
            vmem((total_rows, HD), HALF),
            vmem((total_rows, HD), HALF),
            vmem((resps, 2 * span, HD), HALF),
            vmem((resps, 2 * span, HD), HALF),
            vmem((prompts, both, HD), WIDE),
            vmem((prompts, both, HD), WIDE),
            dma((13,)),
            dma,
            dma,
            dma,
            dma((2,)),
            dma,
            dma((stages,)),
            dma((stages,)),
            dma,
            dma((2,)),
            dma,
            dma,
            dma((7,)),
        ],
        compiler_params=pltpu.CompilerParams(
            collective_id=0, has_side_effects=True, vmem_limit_bytes=48 * 1024 * 1024
        ),
    )(
        prompt_of,
        lengths,
        in_hbm(queries[0]),
        in_hbm(outputs[0]),
        in_hbm(out_grads[0]),
        in_hbm(resp_keys[0]),
        in_hbm(resp_values[0]),
        in_hbm(prompt_keys),
        in_hbm(prompt_values),
    )
    return dq[None], dkv[0][None], dkv[1][None], dpkv[0], dpkv[1]


def solution(mesh):
    sizes = (mesh.shape["heads"], mesh.shape["resp"], mesh.shape["prompt"])
    return jax.shard_map(
        functools.partial(on_device, sizes),
        mesh=mesh,
        in_specs=(
            P(("resp", "prompt"), "heads", None),
            P(("resp", "prompt"), "heads", None),
            P(("resp", "prompt"), "heads", None),
            P(("resp", "prompt"), "heads", None),
            P(("resp", "prompt"), "heads", None),
            P(("resp", "prompt"), None, "heads"),
            P(("resp", "prompt"), None, "heads"),
            P(("resp", "prompt")),
            P(("resp", "prompt")),
        ),
        out_specs=(
            P(("resp", "prompt"), "heads", None),
            P(("resp", "prompt"), "heads", None),
            P(("resp", "prompt"), "heads", None),
            P(("resp", "prompt"), None, "heads"),
            P(("resp", "prompt"), None, "heads"),
        ),
        check_vma=False,
    )
```
